32 devices in a mesh: phi: 8 (over z, x), row: 4 (over y, core).
Axes of the slice: x: 2, y: 2, z: 4, core: 2. Of those that a mesh axis runs over, the one named last changes fastest.
Arguments:
- density: float32 [128, 32, 512], P('phi', None, 'row'), may hold values from 0.5 to 2
- velocity: float32 [3, 128, 32, 512], P(None, 'phi', None, 'row'), may hold values from -0.3 to 0.3
- shifts: int32 [64], P('row'), may hold values from 0 to 31, as said below
- fractions: float32 [64], P('row'), may hold values from 0 to 1
Outputs:
- density_out: float32 [128, 32, 512], P('phi', None, 'row')
- stepped_velocity: float32 [3, 128, 32, 512], P(None, 'phi', None, 'row')
- image: float32 [1024, 1024], P(('phi', 'row'))
The draws below stay inside these ranges and needn't reach their ends.
Inputs may be any that keep to these rules, and one draw needn't show every extreme that they name: `shifts`: some band has shift 0 and some band has shift 32 - 1.
All inputs are finite; a program needn't handle non-finite values.
Results may differ from the reference program's by a relative error of at most 0.000071.
Values sent between devices are 32-bit elements; how exact they have to be, the bound alone decides.
No kernel may reach another device: no remote copies, remote signals or barrier semaphores. Data moves between devices by JAX's collectives and lax.ppermute only.
A program may use at most 64 MiB of HBM per device.

```python
import jax
import jax.numpy as jnp
from jax import lax

NTH = 32
BAND = 8
STEPS = 2
NPIX = 1024
NPHI = 128
NR = 512
NBANDS = 64
SHIFT_MAX = 32


def draw_shifts(key, part):
    first, second, third = jax.random.split(jax.random.fold_in(key, 17), 3)
    values = jax.random.randint(first, (NBANDS,), 0, SHIFT_MAX)
    top = jax.random.randint(second, (), 0, NBANDS)
    low = (top + 1 + jax.random.randint(third, (), 0, NBANDS - 1)) % NBANDS
    values = values.at[top].set(SHIFT_MAX - 1)
    values = values.at[low].set(0)
    return values.astype(jnp.int32)


def shard_levels(stream_key, extent, shards, low, high):
    loudness = 1.0
    for position, shards_of in shards:
        steps = jax.random.uniform(jax.random.fold_in(jax.random.fold_in(stream_key, 6), position), (shards_of,), jnp.float32, low / len(shards), high / len(shards))
        loudness = loudness * jnp.repeat(jnp.exp(steps), extent[position] // shards_of).reshape((-1,) + (1,) * (len(extent) - 1 - position))
    return loudness


def setup_inputs(seed: int = 0) -> dict:
    splits = jax.random.split(jax.random.key(seed), 5)
    return {
        "density": jnp.clip(0.5 + 1.5 * jax.random.uniform(splits[0], (NPHI, NTH, NR), jnp.float32) ** shard_levels(splits[0], (NPHI, NTH, NR), ((0, 8), (2, 4)), -0.2, 0.2), 0.5, 2.0),
        "velocity": jnp.clip(jax.random.uniform(splits[1], (3, NPHI, NTH, NR), jnp.float32, -0.3, 0.3) * shard_levels(splits[1], (3, NPHI, NTH, NR), ((1, 8), (3, 4)), -0.4, 0.0), -0.3, 0.3),
        "shifts": draw_shifts(jax.random.fold_in(splits[4], 71), 0),
        "fractions": jnp.clip(1.0 * jax.random.uniform(splits[3], (NBANDS,), jnp.float32) ** shard_levels(splits[3], (NBANDS,), ((0, 4),), -0.2, 0.2), 0.0, 1.0),
    }


SPEED = 1.5
COURANT = 0.05
KAPPA = 1.5
R_INNER = 0.2

def conserved(prim):
    rho = prim[0]
    return jnp.stack([rho, rho * prim[1], rho * prim[2], rho * prim[3]])

def divergence(extended, axis, comp):
    cons = conserved(extended)
    flux = cons * extended[comp][None]
    flux = flux.at[comp].add(extended[0])
    size = extended.shape[axis]
    low_c = lax.slice_in_dim(cons, 0, size - 1, axis=axis)
    high_c = lax.slice_in_dim(cons, 1, size, axis=axis)
    low_f = lax.slice_in_dim(flux, 0, size - 1, axis=axis)
    high_f = lax.slice_in_dim(flux, 1, size, axis=axis)
    face = 0.5 * (low_f + high_f) - 0.5 * SPEED * (high_c - low_c)
    return lax.slice_in_dim(face, 1, size - 1, axis=axis) - lax.slice_in_dim(face, 0, size - 2, axis=axis)

def advance(prim, ext_phi, padded_polar_grid, ext_radial):
    total = divergence(ext_phi, 1, 2) + divergence(padded_polar_grid, 2, 3) + divergence(ext_radial, 3, 1)
    fresh = conserved(prim) - COURANT * total
    rho = fresh[0]
    return jnp.stack([rho, fresh[1] / rho, fresh[2] / rho, fresh[3] / rho])

def column_light(rho, radial_index, total_radial):
    polar = rho.shape[1]
    dtau = KAPPA / polar * rho
    above = jnp.cumsum(dtau, axis=1) - dtau
    theta = (jnp.arange(polar, dtype=jnp.int32).astype(jnp.float32) + 0.5) / polar
    tilt = 1.0 + 0.5 * jnp.cos(jnp.pi * theta)
    radius = R_INNER + (radial_index.astype(jnp.float32) + 0.5) * (1.0 - R_INNER) / total_radial
    source = (1.0 / jnp.sqrt(radius))[None, None, :] * tilt[None, :, None]
    return lax.optimization_barrier(jnp.sum(source * (1.0 - jnp.exp(-dtau)) * jnp.exp(-above), axis=1))

def pixel_corners(pixel_rows, npix, nphi, nrad):
    yy = ((pixel_rows.astype(jnp.float32) + 0.5) / npix * 2.0 - 1.0)[:, None]
    xx = ((jnp.arange(npix, dtype=jnp.int32).astype(jnp.float32) + 0.5) / npix * 2.0 - 1.0)[None, :]
    dist = jnp.sqrt(xx * xx + yy * yy)
    upos = (dist - R_INNER) / (1.0 - R_INNER) * nrad - 0.5
    radial_floor_index = jnp.floor(upos)
    radial_fraction = upos - radial_floor_index
    radial_lower_index = radial_floor_index.astype(jnp.int32)
    angle = jnp.arctan2(yy, xx)
    vpos = (angle + jnp.pi) / (2.0 * jnp.pi) * nphi - 0.5
    lfloor = jnp.floor(vpos)
    polar_fraction = vpos - lfloor
    polar_lower_index = lfloor.astype(jnp.int32) % nphi
    polar_upper_index = (polar_lower_index + 1) % nphi
    return [(polar_lower_index, radial_lower_index, (1.0 - polar_fraction) * (1.0 - radial_fraction)), (polar_upper_index, radial_lower_index, polar_fraction * (1.0 - radial_fraction)), (polar_lower_index, radial_lower_index + 1, (1.0 - polar_fraction) * radial_fraction), (polar_upper_index, radial_lower_index + 1, polar_fraction * radial_fraction)]

def sample_block(table, corners, l_first, k_first):
    nl, nk = table.shape
    flat = table.reshape(-1)
    total = jnp.zeros(corners[0][2].shape, table.dtype)
    for lidx, kidx, weight in corners:
        lloc = lidx - l_first
        kloc = kidx - k_first
        valid = (lloc >= 0) & (lloc < nl) & (kloc >= 0) & (kloc < nk)
        spot = jnp.clip(lloc, 0, nl - 1) * nk + jnp.clip(kloc, 0, nk - 1)
        total = total + jnp.where(valid, weight * jnp.take(flat, spot), 0.0)
    return total

def reference(density, velocity, shifts, fractions):
    prim = jnp.concatenate([density[None], velocity], axis=0)
    nphi = prim.shape[1]
    nrad = prim.shape[3]
    shift_col = jnp.repeat(shifts, BAND)
    frac_col = jnp.repeat(fractions, BAND)
    cells = jnp.arange(nphi, dtype=jnp.int32)[:, None]
    src_a = (cells - shift_col[None, :]) % nphi
    src_b = (cells - shift_col[None, :] - 1) % nphi
    idx_a = jnp.broadcast_to(src_a[None, :, None, :], prim.shape)
    idx_b = jnp.broadcast_to(src_b[None, :, None, :], prim.shape)
    for step in range(STEPS):
        ext_phi = jnp.pad(prim, ((0, 0), (1, 1), (0, 0), (0, 0)), mode='wrap')
        padded_polar_grid = jnp.pad(prim, ((0, 0), (0, 0), (1, 1), (0, 0)))
        ext_radial = jnp.pad(prim, ((0, 0), (0, 0), (0, 0), (1, 1)))
        prim = advance(prim, ext_phi, padded_polar_grid, ext_radial)
        prim = (1.0 - frac_col) * jnp.take_along_axis(prim, idx_a, axis=1) + frac_col * jnp.take_along_axis(prim, idx_b, axis=1)
    intensity = column_light(prim[0], jnp.arange(nrad, dtype=jnp.int32), nrad)
    corners = pixel_corners(jnp.arange(NPIX, dtype=jnp.int32), NPIX, nphi, nrad)
    image = sample_block(intensity, corners, 0, 0)
    return (prim[0], prim[1:], image)
```

```python
import functools

import jax
import jax.numpy as jnp
import numpy as np
from jax import lax
from jax.experimental import pallas as pl
from jax.experimental.pallas import tpu as pltpu
from jax.sharding import PartitionSpec as P

BAND = 8
STEPS = 2
NPIX = 1024


SPEED = 1.5
COURANT = 0.05
KAPPA = 1.5
R_INNER = 0.2

FIELDS = 4
INNER = 8
HALO = STEPS
LANES = 128
VMEM_LIMIT = 48 * 1024 * 1024


def params():
    return pltpu.CompilerParams(vmem_limit_bytes=VMEM_LIMIT)


def vmem(count):
    return [pl.BlockSpec(memory_space=pltpu.VMEM)] * count


def smem(count):
    return [pl.BlockSpec(memory_space=pltpu.SMEM)] * count


def field_ref(density_ref, velocity_ref, field):
    return density_ref if field == 0 else velocity_ref.at[field - 1]


def pack_kernel(density_ref, velocity_ref, rows_ref):
    cells, polar, radial = density_ref.shape
    groups = polar // INNER
    for field in range(FIELDS):
        source = field_ref(density_ref, velocity_ref, field)
        for group in range(groups):
            block = source[:, pl.ds(group, INNER, stride=groups), :]
            turned = block.reshape(cells * INNER, radial).T
            rows_ref[pl.ds(field * groups + group, radial, stride=FIELDS * groups), :] = turned


def unpack_kernel(rows_ref, density_ref, velocity_ref):
    cells, polar, radial = density_ref.shape
    groups = polar // INNER
    for field in range(FIELDS):
        target = field_ref(density_ref, velocity_ref, field)
        for group in range(groups):
            turned = rows_ref[pl.ds(field * groups + group, radial, stride=FIELDS * groups), :]
            block = turned.T.reshape(cells, INNER, radial)
            target[:, pl.ds(group, INNER, stride=groups), :] = block


def evolve_kernel(cells, cycle, columns, nrad, groups, swap, shift_ref, frac_ref, place_ref, tilt_ref, in_ref, out_ref, light_ref, work_ref, lit_ref):
    extended = columns + 2 * HALO
    per_column = FIELDS * groups
    first = place_ref[0]
    first_global = place_ref[1]
    lane = lax.broadcasted_iota(jnp.int32, (cycle, LANES), 1)
    inner = lane % INNER

    def upper_azimuth(x):
        z = pltpu.roll(x, LANES - INNER, 1)
        return jnp.where(lane < LANES - INNER, z, pltpu.roll(z, cycle - 1, 0))

    def lower_azimuth(x):
        z = pltpu.roll(x, INNER, 1)
        return jnp.where(lane >= INNER, z, pltpu.roll(z, 1, 0))

    def upper_polar(x):
        last = jnp.where(inner == INNER - 1, 0.0, pltpu.roll(x[0], LANES - 1, 1))
        return x[1:] + [last]

    def lower_polar(x):
        head = jnp.where(inner == 0, 0.0, pltpu.roll(x[-1], 1, 1))
        return [head] + x[:-1]

    def conserved(prim):
        return [prim[0]] + [[r * v for r, v in zip(prim[0], prim[k])] for k in (1, 2, 3)]

    half = 0.5 * COURANT
    damp = 0.5 * SPEED * COURANT

    def face_part(cons, speed, comp, sign):
        factor = [half * u + sign * damp for u in speed]
        parts = [[c * m for c, m in zip(cons[k], factor)] for k in range(FIELDS)]
        parts[comp] = [p + half * r for p, r in zip(parts[comp], cons[0])]
        return parts

    def contributions(prim):
        cons = conserved(prim)
        a_phi = face_part(cons, prim[2], 2, -1.0)
        b_phi = face_part(cons, prim[2], 2, 1.0)
        a_th = face_part(cons, prim[3], 3, -1.0)
        b_th = face_part(cons, prim[3], 3, 1.0)
        keep = 1.0 - 3.0 * SPEED * COURANT
        pend = []
        for k in range(FIELDS):
            up_t = upper_polar(a_th[k])
            low_t = lower_polar(b_th[k])
            pend.append([
                keep * cons[k][g] - (upper_azimuth(a_phi[k][g]) - lower_azimuth(b_phi[k][g])) - (up_t[g] - low_t[g])
                for g in range(groups)
            ])
        return pend, face_part(cons, prim[1], 1, -1.0), face_part(cons, prim[1], 1, 1.0)

    def combine(x, y, sign):
        return [[p + sign * q for p, q in zip(a, b)] for a, b in zip(x, y)]

    def finish(fresh, col):
        number = first_global + col - HALO
        valid = (number >= 0) & (number < nrad)
        band = (first + col - HALO + BAND) // BAND
        shift = shift_ref[band]
        weight = frac_ref[band]
        turn = shift // cells
        step = INNER * (shift % cells)
        inside = lane >= step
        inverse = [1.0 / r for r in fresh[0]]
        prim = [fresh[0]] + [[m * i for m, i in zip(fresh[k], inverse)] for k in (1, 2, 3)]
        moved = []
        for k in range(FIELDS):
            row = []
            for x in prim[k]:
                x = jnp.where(valid, x, 0.0)
                x = (1.0 - weight) * x + weight * lower_azimuth(x)
                z = pltpu.roll(x, step, 1)
                z = jnp.where(inside, z, pltpu.roll(z, 1, 0))
                row.append(pltpu.roll(z, turn, 0))
            moved.append(row)
        return moved

    def step_columns(read, write, low, high):
        prim = read(low)
        before = face_part(conserved(prim), prim[1], 1, 1.0)
        pend, _, after = contributions(read(low + 1))
        pend = combine(pend, before, 1.0)

        def body(col, carry):
            pend, before = carry
            fresh_pend, a_rad, b_rad = contributions(read(col))
            write(col - 1, finish(combine(pend, a_rad, -1.0), col - 1))
            return combine(fresh_pend, before, 1.0), b_rad

        pend, _ = lax.fori_loop(low + 2, high - 1, body, (pend, after))
        prim = read(high - 1)
        a_rad = face_part(conserved(prim), prim[1], 1, -1.0)
        write(high - 2, finish(combine(pend, a_rad, -1.0), high - 2))

    def read_input(col):
        return [
            [in_ref[pl.ds(col * per_column + k * groups + g, cycle, stride=extended * per_column), :] for g in range(groups)]
            for k in range(FIELDS)
        ]

    def read_work(col):
        return [[work_ref[col * per_column + k * groups + g] for g in range(groups)] for k in range(FIELDS)]

    def write_work(col, prim):
        for k in range(FIELDS):
            for g in range(groups):
                work_ref[col * per_column + k * groups + g] = prim[k][g]

    def write_output(col, prim):
        own = col - HALO
        for k in range(FIELDS):
            for g in range(groups):
                out_ref[pl.ds(own * per_column + k * groups + g, cycle, stride=columns * per_column), :] = prim[k][g]
        dtau = [(KAPPA / (groups * INNER)) * r for r in prim[0]]
        total = dtau[0]
        for d in dtau[1:]:
            total = total + d
        run = total
        for d in (1, 2, 4):
            run = run + jnp.where(inner >= d, pltpu.roll(run, d, 1), 0.0)
        above = run - total
        light = jnp.zeros_like(total)
        for g in range(groups):
            light = light + tilt_ref[pl.ds(g, 1), :] * (1.0 - jnp.exp(-dtau[g])) * jnp.exp(-above)
            above = above + dtau[g]
        for d in (1, 2, 4):
            light = light + pltpu.roll(light, LANES - d, 1)
        number = jnp.full((cycle, LANES), first_global + own, jnp.int32).astype(jnp.float32)
        radius = R_INNER + (number + 0.5) * (1.0 - R_INNER) / nrad
        light = light * (1.0 / jnp.sqrt(radius))
        slot = own % INNER
        light = pltpu.roll(light, slot, 1)
        lit_ref[own // INNER] = jnp.where(inner == slot, light, lit_ref[own // INNER])

    lit_ref[...] = jnp.zeros_like(lit_ref)
    step_columns(read_input, write_work, 0, extended)
    step_columns(read_work, write_output, 1, extended - 1)
    if swap:
        sub = lax.broadcasted_iota(jnp.int32, (cycle, LANES), 0)
        for h in range(columns // INNER):
            x = lit_ref[h]
            for d in (1, 2, 4):
                low_sub = (sub & d) == 0
                low_lane = (lane & d) == 0
                ahead = pltpu.roll(pltpu.roll(x, cycle - d, 0), d, 1)
                back = pltpu.roll(pltpu.roll(x, d, 0), LANES - d, 1)
                x = jnp.where(low_sub == low_lane, x, jnp.where(low_sub, ahead, back))
            light_ref[pl.ds(h * INNER, INNER), :] = x
    else:
        light_ref[...] = lit_ref[...]


def pixel_tiles(first_row, rows_dev, npix, nphi, nrad):
    tile_rows = min(8, rows_dev)
    tile_cols = LANES // tile_rows
    across = npix // tile_cols
    tiles = rows_dev // tile_rows * across
    tile = lax.broadcasted_iota(jnp.int32, (tiles, LANES), 0)
    pixel = lax.broadcasted_iota(jnp.int32, (tiles, LANES), 1)
    row = first_row + tile // across * tile_rows + pixel // tile_cols
    col = tile % across * tile_cols + pixel % tile_cols
    yy = (row.astype(jnp.float32) + 0.5) / npix * 2.0 - 1.0
    xx = (col.astype(jnp.float32) + 0.5) / npix * 2.0 - 1.0
    dist = jnp.sqrt(xx * xx + yy * yy)
    upos = (dist - R_INNER) / (1.0 - R_INNER) * nrad - 0.5
    floor_u = jnp.floor(upos)
    frac_u = upos - floor_u
    lower = jnp.clip(floor_u.astype(jnp.int32), -2, nrad) + LANES
    angle = jnp.arctan2(yy, xx)
    vpos = (angle + jnp.pi) / (2.0 * jnp.pi) * nphi - 0.5
    window = jnp.min(lower, axis=1) // (LANES // 2)
    window = jnp.clip(window, 0, (nrad + LANES) // (LANES // 2))
    start = jnp.clip(jnp.floor(jnp.min(vpos, axis=1)).astype(jnp.int32) + 8, 0, nphi + 8)
    spot = jnp.clip(lower - window[:, None] * (LANES // 2), 0, LANES - 2)
    return start, window, spot, frac_u, vpos + 8.0 - start[:, None].astype(jnp.float32)


def window_rows(rows_dev, npix, nphi):
    tile_rows = min(8, rows_dev)
    tile_cols = LANES // tile_rows
    diagonal = 2.0 * np.hypot(tile_rows, tile_cols) / npix
    span = diagonal / (R_INNER - diagonal) / (2.0 * np.pi) * nphi
    return -(-int(np.ceil(span) + 2) // 8) * 8


def image_kernel(cells, cycle, nphi, nrad, rows, tile_rows, across, start_ref, window_ref, table_ref, spot_ref, frac_ref, vpos_ref, out_ref, turned_ref, wide_ref):
    blocks = nrad // LANES
    for k in range(blocks):
        for l in range(nphi // LANES):
            turned_ref[pl.ds(k * nphi + l * LANES, LANES), :] = table_ref[
                pl.ds(k * LANES, LANES), pl.ds(l * LANES, LANES)
            ].T
    half = LANES // 2
    windows = 2 * (blocks + 2) - 1
    tall = wide_ref.shape[0] // windows

    def fill(s, carry):
        zero = jnp.zeros((cells, LANES), jnp.float32)
        value = [zero] + [turned_ref[pl.ds(k * nphi + s, cells, stride=cycle), :] for k in range(blocks)] + [zero]
        for w in range(windows):
            piece = value[w // 2]
            if w % 2:
                piece = jnp.concatenate([piece[:, half:], value[w // 2 + 1][:, :half]], axis=1)
            wide_ref[pl.ds((8 + s * cells) * windows + w, cells, stride=windows), :] = piece
        return carry

    lax.fori_loop(0, cycle, fill, 0)
    pad = tall - nphi - 8
    wide_ref[pl.ds(0, 8 * windows), :] = wide_ref[pl.ds(nphi * windows, 8 * windows), :]
    wide_ref[pl.ds((nphi + 8) * windows, pad * windows), :] = wide_ref[pl.ds(8 * windows, pad * windows), :]

    sub = lax.broadcasted_iota(jnp.int32, (8, LANES), 0)
    lane = lax.broadcasted_iota(jnp.int32, (8, LANES), 1)

    def one_tile(tile):
        start = start_ref[tile]
        at = start * windows + window_ref[tile]
        spot = jnp.broadcast_to(spot_ref[pl.ds(tile, 1), :], (8, LANES))
        frac = jnp.broadcast_to(frac_ref[pl.ds(tile, 1), :], (8, LANES))
        vpos = jnp.broadcast_to(vpos_ref[pl.ds(tile, 1), :], (8, LANES))
        total = None
        for r in range(0, rows, 8):
            block = wide_ref[pl.ds(at + r * windows, 8, stride=windows), :]
            low = jnp.take_along_axis(block, spot, axis=1)
            high = jnp.take_along_axis(block, spot + 1, axis=1)
            weight = jnp.maximum(0.0, 1.0 - jnp.abs((sub + r).astype(jnp.float32) - vpos))
            part = weight * (low + frac * (high - low))
            total = part if total is None else total + part
        for d in (4, 2, 1):
            total = total + pltpu.roll(total, d, 0)
        return total

    def group(index, carry):
        result = jnp.zeros((8, LANES), jnp.float32)
        for t in range(8):
            result = jnp.where(sub == t, one_tile(index * 8 + t), result)
        if tile_rows == 8:
            width = LANES // 8
            for d in (1, 2, 4):
                low_sub = (sub & d) == 0
                low_lane = (lane & (d * width)) == 0
                ahead = pltpu.roll(pltpu.roll(result, 8 - d, 0), d * width, 1)
                back = pltpu.roll(pltpu.roll(result, d, 0), LANES - d * width, 1)
                result = jnp.where(low_sub == low_lane, result, jnp.where(low_sub, ahead, back))
            per_row = across // 8
            out_ref[pl.ds(pl.multiple_of(index // per_row * 8, 8), 8), pl.ds(pl.multiple_of(index % per_row * LANES, LANES), LANES)] = result
        else:
            out_ref[pl.ds(pl.multiple_of(index * 8, 8), 8), :] = result
        return carry

    lax.fori_loop(0, spot_ref.shape[0] // 8, group, 0)


def draw_image(table, geometry, cells, cycle, rows_dev, npix, nphi, nrad):
    start, window, spot, frac_u, vpos = geometry
    tiles = spot.shape[0]
    tile_rows = min(8, rows_dev)
    tile_cols = LANES // tile_rows
    across = npix // tile_cols
    rows = window_rows(rows_dev, npix, nphi)
    windows = 2 * (nrad // LANES + 2) - 1
    shape = (rows_dev, npix) if tile_rows == 8 else (tiles, LANES)
    image = pl.pallas_call(
        functools.partial(image_kernel, cells, cycle, nphi, nrad, rows, tile_rows, across),
        out_shape=jax.ShapeDtypeStruct(shape, jnp.float32),
        in_specs=smem(2) + vmem(4),
        out_specs=pl.BlockSpec(memory_space=pltpu.VMEM),
        scratch_shapes=[
            pltpu.VMEM((nphi * (nrad // LANES), LANES), jnp.float32),
            pltpu.VMEM(((nphi + 16 + rows) * windows, LANES), jnp.float32),
        ],
        compiler_params=params(),
        name="image",
    )(start, window, table, spot, frac_u, vpos)
    if tile_rows == 8:
        return image
    image = image.reshape(rows_dev // tile_rows, across, tile_rows, tile_cols)
    return jnp.swapaxes(image, 1, 2).reshape(rows_dev, npix)


def body(density, velocity, shifts, fractions):
    cycle = lax.axis_size("phi")
    bands = lax.axis_size("row")
    cells, polar, radial = density.shape
    groups = polar // INNER
    per_column = FIELDS * groups
    columns = radial // cycle
    extended = columns + 2 * HALO
    nphi = cells * cycle
    nrad = radial * bands
    place = lax.axis_index("phi")
    row = lax.axis_index("row")

    rows = pl.pallas_call(
        pack_kernel,
        out_shape=jax.ShapeDtypeStruct((radial * per_column, LANES), jnp.float32),
        in_specs=vmem(2),
        out_specs=pl.BlockSpec(memory_space=pltpu.VMEM),
        compiler_params=params(),
        name="pack",
    )(density, velocity)
    edge = HALO * per_column

    def with_band(block, band):
        extra = jnp.stack([shifts[band].astype(jnp.float32), fractions[band]])
        return jnp.concatenate([block, jnp.pad(extra[:, None], ((0, 6), (0, LANES - 1)))])

    left = lax.ppermute(with_band(rows[-edge:], -1), "row", [(i, i + 1) for i in range(bands - 1)])
    right = lax.ppermute(with_band(rows[:edge], 0), "row", [(i + 1, i) for i in range(bands - 1)])
    ext_shift = jnp.concatenate([left[edge, :1].astype(jnp.int32), shifts, right[edge, :1].astype(jnp.int32)])
    ext_frac = jnp.concatenate([left[edge + 1, :1], fractions, right[edge + 1, :1]])
    rows = jnp.concatenate([left[:edge], rows, right[:edge]])
    stride = columns * per_column
    chunks = jnp.stack([rows[q * stride:q * stride + extended * per_column] for q in range(cycle)])
    ring = lax.all_to_all(chunks, "phi", 0, 0, tiled=True)

    swap = cycle == INNER and columns % INNER == 0
    slots = -(-columns // INNER)
    theta = (np.arange(polar) + 0.5) / polar
    tilt = (1.0 + 0.5 * np.cos(np.pi * theta)).reshape(INNER, groups).T
    tilt = jnp.asarray(np.tile(tilt, (1, LANES // INNER)), jnp.float32)
    where = jnp.stack([place * columns, row * radial + place * columns])
    rows, light = pl.pallas_call(
        functools.partial(evolve_kernel, cells, cycle, columns, nrad, groups, swap),
        out_shape=(
            jax.ShapeDtypeStruct((cycle * columns * per_column, LANES), jnp.float32),
            jax.ShapeDtypeStruct((columns, LANES) if swap else (slots, cycle, LANES), jnp.float32),
        ),
        in_specs=smem(3) + vmem(2),
        out_specs=tuple(vmem(2)),
        scratch_shapes=[
            pltpu.VMEM((extended * per_column, cycle, LANES), jnp.float32),
            pltpu.VMEM((slots, cycle, LANES), jnp.float32),
        ],
        compiler_params=params(),
        name="evolve",
    )(ext_shift, ext_frac, where, tilt, ring.reshape(cycle * extended * per_column, LANES))
    if not swap:
        light = light.reshape(slots, cycle, cells, INNER).transpose(0, 3, 2, 1).reshape(slots * INNER, nphi)[:columns]

    table = lax.all_gather(light, "phi", axis=0, tiled=True)
    table = lax.all_gather(table, "row", axis=0, tiled=True)
    back = lax.all_to_all(rows.reshape(cycle, columns * per_column, LANES), "phi", 0, 0, tiled=True)
    density_out, velocity_out = pl.pallas_call(
        unpack_kernel,
        out_shape=(
            jax.ShapeDtypeStruct(density.shape, jnp.float32),
            jax.ShapeDtypeStruct(velocity.shape, jnp.float32),
        ),
        in_specs=vmem(1),
        out_specs=tuple(vmem(2)),
        compiler_params=params(),
        name="unpack",
    )(back.reshape(radial * per_column, LANES))

    rows_dev = NPIX // (cycle * bands)
    first_row = (place * bands + row) * rows_dev
    geometry = pixel_tiles(first_row, rows_dev, NPIX, nphi, nrad)
    image = draw_image(table, geometry, cells, cycle, rows_dev, NPIX, nphi, nrad)
    return (density_out, velocity_out, image)


def solution(mesh):
    in_specs = (P("phi", None, "row"), P(None, "phi", None, "row"), P("row"), P("row"))
    out_specs = (P("phi", None, "row"), P(None, "phi", None, "row"), P(("phi", "row"), None))
    return jax.shard_map(body, mesh=mesh, in_specs=in_specs, out_specs=out_specs, check_vma=False)
```

```python
import functools

import jax
import jax.numpy as jnp
import numpy as np
from jax import lax
from jax.experimental import pallas as pl
from jax.experimental.pallas import tpu as pltpu
from jax.sharding import PartitionSpec as P

BAND = 8
STEPS = 2
NPIX = 1024


SPEED = 1.5
COURANT = 0.05
KAPPA = 1.5
R_INNER = 0.2

FIELDS = 4
INNER = 8
HALO = STEPS
LANES = 128
PARTS = 1
VMEM_LIMIT = 48 * 1024 * 1024


def params():
    return pltpu.CompilerParams(vmem_limit_bytes=VMEM_LIMIT)


def vmem(count):
    return [pl.BlockSpec(memory_space=pltpu.VMEM)] * count


def smem(count):
    return [pl.BlockSpec(memory_space=pltpu.SMEM)] * count


def field_ref(density_ref, velocity_ref, field):
    return density_ref if field == 0 else velocity_ref.at[field - 1]


def pack_kernel(last, shift_ref, frac_ref, density_ref, velocity_ref, rows_ref, left_ref, right_ref, field_refs, arrived):
    cells, polar, radial = density_ref.shape
    groups = polar // INNER
    per_column = FIELDS * groups
    copies = []
    for field in range(FIELDS):
        copy = pltpu.make_async_copy(field_ref(density_ref, velocity_ref, field), field_refs.at[field], arrived.at[field])
        copy.start()
        copies.append(copy)
    for field in range(FIELDS):
        copies[field].wait()
        for group in range(groups):
            block = field_refs[field, :, pl.ds(group, INNER, stride=groups), :]
            turned = block.reshape(cells * INNER, radial).T
            rows_ref[pl.ds(field * groups + group, radial, stride=per_column), :] = turned
    edge = HALO * per_column
    sub = lax.broadcasted_iota(jnp.int32, (8, LANES), 0)
    for ref, at, band in ((left_ref, 0, 0), (right_ref, radial * per_column - edge, last)):
        ref[pl.ds(0, edge), :] = rows_ref[pl.ds(at, edge), :]
        ref[pl.ds(edge, 8), :] = jnp.where(sub == 0, shift_ref[band].astype(jnp.float32), frac_ref[band])


def chunk_kernel(cycle, spans, place_ref, rows_ref, left_ref, right_ref, *chunk_refs):
    edge = left_ref.shape[0] - 8
    per_column = edge // HALO
    stride = rows_ref.shape[0] // cycle
    place = place_ref[0]
    for j in range(cycle):
        owner = place ^ j
        for part, (low, high) in enumerate(spans):
            target = chunk_refs[part * cycle + j]
            for col in range(low, high):
                at = (col - HALO) * per_column
                slot = pl.ds((col - low) * per_column, per_column)
                start = pl.multiple_of(jnp.clip(owner * stride + at, 0, rows_ref.shape[0] - per_column), per_column)
                value = rows_ref[pl.ds(start, per_column), :]
                if col < HALO:
                    value = jnp.where(owner == 0, left_ref[pl.ds(col * per_column, per_column), :], value)
                if at >= stride:
                    value = jnp.where(owner == cycle - 1, right_ref[pl.ds(at - stride, per_column), :], value)
                target[slot, :] = value


def unpack_kernel(cycle, spans, place_ref, *refs):
    count = len(spans) * cycle
    chunk_refs = refs[:count]
    density_ref, velocity_ref, rows_ref, field_refs, leaving = refs[count:]
    cells, polar, radial = density_ref.shape
    groups = polar // INNER
    per_column = FIELDS * groups
    stride = radial // cycle * per_column
    place = place_ref[0]
    for j in range(cycle):
        owner = place ^ j
        for part, (low, high) in enumerate(spans):
            size = (high - low) * per_column
            at = pl.multiple_of(owner * stride + low * per_column, per_column)
            rows_ref[pl.ds(at, size), :] = chunk_refs[part * cycle + j][...]
    copies = []
    for field in range(FIELDS):
        for group in range(groups):
            turned = rows_ref[pl.ds(field * groups + group, radial, stride=per_column), :]
            block = turned.T.reshape(cells, INNER, radial)
            field_refs[field, :, pl.ds(group, INNER, stride=groups), :] = block
        copy = pltpu.make_async_copy(field_refs.at[field], field_ref(density_ref, velocity_ref, field), leaving.at[field])
        copy.start()
        copies.append(copy)
    for copy in copies:
        copy.wait()


def evolve_kernel(cells, cycle, first_column, columns, nrad, groups, segments, shift_ref, frac_ref, place_ref, tilt_ref, *refs):
    extended = columns + 2 * HALO
    per_column = FIELDS * groups
    count = len(segments) * cycle
    chunk_refs = refs[:count]
    out_refs = refs[count:count + cycle]
    light_ref, full_ref, work_ref, done_ref = refs[count + cycle:]
    swap = len(light_ref.shape) == 2
    place = place_ref[0]
    first = place_ref[1] + first_column
    first_global = place_ref[2] + first_column
    for j in range(cycle):
        for index, (low, high, at) in enumerate(segments):
            size = (high - low) * per_column
            full_ref[pl.ds(low * per_column * cycle + (place ^ j), size, stride=cycle), :] = chunk_refs[index * cycle + j][pl.ds(at, size), :]
    lane = lax.broadcasted_iota(jnp.int32, (cycle, LANES), 1)
    inner = lane % INNER

    def upper_azimuth(x):
        z = pltpu.roll(x, LANES - INNER, 1)
        return jnp.where(lane < LANES - INNER, z, pltpu.roll(z, cycle - 1, 0))

    def lower_azimuth(x):
        z = pltpu.roll(x, INNER, 1)
        return jnp.where(lane >= INNER, z, pltpu.roll(z, 1, 0))

    def upper_polar(x):
        last = jnp.where(inner == INNER - 1, 0.0, pltpu.roll(x[0], LANES - 1, 1))
        return x[1:] + [last]

    def lower_polar(x):
        head = jnp.where(inner == 0, 0.0, pltpu.roll(x[-1], 1, 1))
        return [head] + x[:-1]

    def conserved(prim):
        return [prim[0]] + [[r * v for r, v in zip(prim[0], prim[k])] for k in (1, 2, 3)]

    half = 0.5 * COURANT
    damp = 0.5 * SPEED * COURANT

    def face_part(cons, speed, comp, sign):
        factor = [half * u + sign * damp for u in speed]
        parts = [[c * m for c, m in zip(cons[k], factor)] for k in range(FIELDS)]
        parts[comp] = [p + half * r for p, r in zip(parts[comp], cons[0])]
        return parts

    def contributions(prim):
        cons = conserved(prim)
        a_phi = face_part(cons, prim[2], 2, -1.0)
        b_phi = face_part(cons, prim[2], 2, 1.0)
        a_th = face_part(cons, prim[3], 3, -1.0)
        b_th = face_part(cons, prim[3], 3, 1.0)
        keep = 1.0 - 3.0 * SPEED * COURANT
        pend = []
        for k in range(FIELDS):
            up_t = upper_polar(a_th[k])
            low_t = lower_polar(b_th[k])
            pend.append([
                keep * cons[k][g] - (upper_azimuth(a_phi[k][g]) - lower_azimuth(b_phi[k][g])) - (up_t[g] - low_t[g])
                for g in range(groups)
            ])
        return pend, face_part(cons, prim[1], 1, -1.0), face_part(cons, prim[1], 1, 1.0)

    def combine(x, y, sign):
        return [[p + sign * q for p, q in zip(a, b)] for a, b in zip(x, y)]

    def finish(fresh, col):
        number = first_global + col - HALO
        valid = (number >= 0) & (number < nrad)
        band = (first + col - HALO + BAND) // BAND
        shift = shift_ref[band]
        weight = frac_ref[band]
        turn = shift // cells
        step = INNER * (shift % cells)
        inside = lane >= step
        inverse = [1.0 / r for r in fresh[0]]
        prim = [fresh[0]] + [[m * i for m, i in zip(fresh[k], inverse)] for k in (1, 2, 3)]
        moved = []
        for k in range(FIELDS):
            row = []
            for x in prim[k]:
                x = jnp.where(valid, x, 0.0)
                x = (1.0 - weight) * x + weight * lower_azimuth(x)
                z = pltpu.roll(x, step, 1)
                z = jnp.where(inside, z, pltpu.roll(z, 1, 0))
                row.append(pltpu.roll(z, turn, 0))
            moved.append(row)
        return moved

    def step_columns(read, write, low, high):
        prim = read(low)
        before = face_part(conserved(prim), prim[1], 1, 1.0)
        pend, _, after = contributions(read(low + 1))
        pend = combine(pend, before, 1.0)

        def body(col, carry):
            pend, before = carry
            fresh_pend, a_rad, b_rad = contributions(read(col))
            write(col - 1, finish(combine(pend, a_rad, -1.0), col - 1))
            return combine(fresh_pend, before, 1.0), b_rad

        pend, _ = lax.fori_loop(low + 2, high - 1, body, (pend, after), unroll=2)
        prim = read(high - 1)
        a_rad = face_part(conserved(prim), prim[1], 1, -1.0)
        write(high - 2, finish(combine(pend, a_rad, -1.0), high - 2))

    def at(col, k, g):
        return pl.multiple_of((col * per_column + k * groups + g) * cycle, cycle)

    def read_input(col):
        return [[full_ref[pl.ds(at(col, k, g), cycle), :] for g in range(groups)] for k in range(FIELDS)]

    def read_work(col):
        return [[work_ref[pl.ds(at(col, k, g), cycle), :] for g in range(groups)] for k in range(FIELDS)]

    def write_work(col, prim):
        for k in range(FIELDS):
            for g in range(groups):
                work_ref[pl.ds(at(col, k, g), cycle), :] = prim[k][g]

    def write_output(col, prim):
        own = col - HALO
        for k in range(FIELDS):
            for g in range(groups):
                done_ref[pl.ds(at(own, k, g), cycle), :] = prim[k][g]
        dtau = [(KAPPA / (groups * INNER)) * r for r in prim[0]]
        total = dtau[0]
        for d in dtau[1:]:
            total = total + d
        run = total
        for d in (1, 2, 4):
            run = run + jnp.where(inner >= d, pltpu.roll(run, d, 1), 0.0)
        above = run - total
        light = jnp.zeros_like(total)
        for g in range(groups):
            light = light + tilt_ref[pl.ds(g, 1), :] * (1.0 - jnp.exp(-dtau[g])) * jnp.exp(-above)
            above = above + dtau[g]
        for d in (1, 2, 4):
            light = light + pltpu.roll(light, LANES - d, 1)
        number = jnp.full((cycle, LANES), first_global + own, jnp.int32).astype(jnp.float32)
        radius = R_INNER + (number + 0.5) * (1.0 - R_INNER) / nrad
        light = light * (1.0 / jnp.sqrt(radius))
        slot = own % INNER
        light = pltpu.roll(light, slot, 1)
        if swap:
            spot = pl.ds(pl.multiple_of(own // INNER * INNER, INNER), INNER)
            light_ref[spot, :] = jnp.where(inner == slot, light, light_ref[spot, :])
        else:
            light_ref[own // INNER] = jnp.where(inner == slot, light, light_ref[own // INNER])

    light_ref[...] = jnp.zeros_like(light_ref)
    step_columns(read_input, write_work, 0, extended)
    step_columns(read_work, write_output, 1, extended - 1)
    for j in range(cycle):
        out_refs[j][...] = done_ref[pl.ds(place ^ j, columns * per_column, stride=cycle), :]
    if swap:
        sub = lax.broadcasted_iota(jnp.int32, (cycle, LANES), 0)
        for h in range(columns // INNER):
            x = light_ref[pl.ds(h * INNER, INNER), :]
            for d in (1, 2, 4):
                low_sub = (sub & d) == 0
                low_lane = (lane & d) == 0
                ahead = pltpu.roll(pltpu.roll(x, cycle - d, 0), d, 1)
                back = pltpu.roll(pltpu.roll(x, d, 0), LANES - d, 1)
                x = jnp.where(low_sub == low_lane, x, jnp.where(low_sub, ahead, back))
            light_ref[pl.ds(h * INNER, INNER), :] = x


def pixel_tiles(first_row, rows_dev, npix, nphi, nrad):
    tile_rows = min(8, rows_dev)
    tile_cols = LANES // tile_rows
    across = npix // tile_cols
    tiles = rows_dev // tile_rows * across
    tile = lax.broadcasted_iota(jnp.int32, (tiles, LANES), 0)
    pixel = lax.broadcasted_iota(jnp.int32, (tiles, LANES), 1)
    row = first_row + tile // across * tile_rows + pixel // tile_cols
    col = tile % across * tile_cols + pixel % tile_cols
    yy = (row.astype(jnp.float32) + 0.5) / npix * 2.0 - 1.0
    xx = (col.astype(jnp.float32) + 0.5) / npix * 2.0 - 1.0
    dist = jnp.sqrt(xx * xx + yy * yy)
    upos = (dist - R_INNER) / (1.0 - R_INNER) * nrad - 0.5
    floor_u = jnp.floor(upos)
    frac_u = upos - floor_u
    lower = jnp.clip(floor_u.astype(jnp.int32), -2, nrad) + LANES
    angle = jnp.arctan2(yy, xx)
    vpos = (angle + jnp.pi) / (2.0 * jnp.pi) * nphi - 0.5
    window = jnp.min(lower, axis=1) // (LANES // 2)
    window = jnp.clip(window, 0, (nrad + LANES) // (LANES // 2))
    start = jnp.clip(jnp.floor(jnp.min(vpos, axis=1)).astype(jnp.int32) + 8, 0, nphi + 8)
    spot = jnp.clip(lower - window[:, None] * (LANES // 2), 0, LANES - 2)
    return start, window, spot, frac_u, vpos + 8.0 - start[:, None].astype(jnp.float32)


def window_rows(rows_dev, npix, nphi):
    tile_rows = min(8, rows_dev)
    tile_cols = LANES // tile_rows
    diagonal = 2.0 * np.hypot(tile_rows, tile_cols) / npix
    span = diagonal / (R_INNER - diagonal) / (2.0 * np.pi) * nphi
    return -(-int(np.ceil(span) + 2) // 8) * 8


def image_kernel(cells, cycle, nphi, nrad, rows, tile_rows, across, start_ref, window_ref, table_ref, spot_ref, frac_ref, vpos_ref, out_ref, turned_ref, wide_ref):
    blocks = nrad // LANES
    for k in range(blocks):
        for l in range(nphi // LANES):
            turned_ref[pl.ds(k * nphi + l * LANES, LANES), :] = table_ref[
                pl.ds(k * LANES, LANES), pl.ds(l * LANES, LANES)
            ].T
    half = LANES // 2
    windows = 2 * (blocks + 2) - 1
    tall = wide_ref.shape[0] // windows

    def fill(s, carry):
        zero = jnp.zeros((cells, LANES), jnp.float32)
        value = [zero] + [turned_ref[pl.ds(k * nphi + s, cells, stride=cycle), :] for k in range(blocks)] + [zero]
        for w in range(windows):
            piece = value[w // 2]
            if w % 2:
                piece = jnp.concatenate([piece[:, half:], value[w // 2 + 1][:, :half]], axis=1)
            wide_ref[pl.ds((8 + s * cells) * windows + w, cells, stride=windows), :] = piece
        return carry

    lax.fori_loop(0, cycle, fill, 0)
    pad = tall - nphi - 8
    wide_ref[pl.ds(0, 8 * windows), :] = wide_ref[pl.ds(nphi * windows, 8 * windows), :]
    wide_ref[pl.ds((nphi + 8) * windows, pad * windows), :] = wide_ref[pl.ds(8 * windows, pad * windows), :]

    sub = lax.broadcasted_iota(jnp.int32, (8, LANES), 0)
    lane = lax.broadcasted_iota(jnp.int32, (8, LANES), 1)

    def one_tile(tile):
        start = start_ref[tile]
        at = start * windows + window_ref[tile]
        spot = jnp.broadcast_to(spot_ref[pl.ds(tile, 1), :], (8, LANES))
        frac = jnp.broadcast_to(frac_ref[pl.ds(tile, 1), :], (8, LANES))
        vpos = jnp.broadcast_to(vpos_ref[pl.ds(tile, 1), :], (8, LANES))
        total = None
        for r in range(0, rows, 8):
            block = wide_ref[pl.ds(at + r * windows, 8, stride=windows), :]
            low = jnp.take_along_axis(block, spot, axis=1)
            high = jnp.take_along_axis(block, spot + 1, axis=1)
            weight = jnp.maximum(0.0, 1.0 - jnp.abs((sub + r).astype(jnp.float32) - vpos))
            part = weight * (low + frac * (high - low))
            total = part if total is None else total + part
        for d in (4, 2, 1):
            total = total + pltpu.roll(total, d, 0)
        return total

    def group(index, carry):
        result = jnp.zeros((8, LANES), jnp.float32)
        for t in range(8):
            result = jnp.where(sub == t, one_tile(index * 8 + t), result)
        if tile_rows == 8:
            width = LANES // 8
            for d in (1, 2, 4):
                low_sub = (sub & d) == 0
                low_lane = (lane & (d * width)) == 0
                ahead = pltpu.roll(pltpu.roll(result, 8 - d, 0), d * width, 1)
                back = pltpu.roll(pltpu.roll(result, d, 0), LANES - d * width, 1)
                result = jnp.where(low_sub == low_lane, result, jnp.where(low_sub, ahead, back))
            per_row = across // 8
            out_ref[pl.ds(pl.multiple_of(index // per_row * 8, 8), 8), pl.ds(pl.multiple_of(index % per_row * LANES, LANES), LANES)] = result
        else:
            out_ref[pl.ds(pl.multiple_of(index * 8, 8), 8), :] = result
        return carry

    lax.fori_loop(0, spot_ref.shape[0] // 8, group, 0)


def draw_image(table, geometry, cells, cycle, rows_dev, npix, nphi, nrad):
    start, window, spot, frac_u, vpos = geometry
    tiles = spot.shape[0]
    tile_rows = min(8, rows_dev)
    tile_cols = LANES // tile_rows
    across = npix // tile_cols
    rows = window_rows(rows_dev, npix, nphi)
    windows = 2 * (nrad // LANES + 2) - 1
    shape = (rows_dev, npix) if tile_rows == 8 else (tiles, LANES)
    image = pl.pallas_call(
        functools.partial(image_kernel, cells, cycle, nphi, nrad, rows, tile_rows, across),
        out_shape=jax.ShapeDtypeStruct(shape, jnp.float32),
        in_specs=smem(2) + vmem(4),
        out_specs=pl.BlockSpec(memory_space=pltpu.VMEM),
        scratch_shapes=[
            pltpu.VMEM((nphi * (nrad // LANES), LANES), jnp.float32),
            pltpu.VMEM(((nphi + 16 + rows) * windows, LANES), jnp.float32),
        ],
        compiler_params=params(),
        name="image",
    )(start, window, table, spot, frac_u, vpos)
    if tile_rows == 8:
        return image
    image = image.reshape(rows_dev // tile_rows, across, tile_rows, tile_cols)
    return jnp.swapaxes(image, 1, 2).reshape(rows_dev, npix)


def exchange(chunks, axis):
    size = lax.axis_size(axis)
    far_first = sorted(range(1, size), reverse=True)
    got = {j: lax.ppermute(chunks[j], axis, [(i, i ^ j) for i in range(size)]) for j in far_first}
    return [chunks[0]] + [got[j] for j in range(1, size)]


def gather_kernel(size, place_ref, *refs):
    out_ref = refs[size]
    count = refs[0].shape[0]
    for j in range(size):
        out_ref[pl.ds(pl.multiple_of((place_ref[0] ^ j) * count, count), count), :] = refs[j][...]


def body(density, velocity, shifts, fractions):
    cycle = lax.axis_size("phi")
    bands = lax.axis_size("row")
    cells, polar, radial = density.shape
    groups = polar // INNER
    per_column = FIELDS * groups
    columns = radial // cycle
    nphi = cells * cycle
    nrad = radial * bands
    place = lax.axis_index("phi")
    row = lax.axis_index("row")
    where = jnp.stack([place, place * columns, row * radial + place * columns])
    block = (FIELDS, cells, polar, radial)

    edge = HALO * per_column
    rows, left, right = pl.pallas_call(
        functools.partial(pack_kernel, shifts.shape[0] - 1),
        out_shape=(
            jax.ShapeDtypeStruct((radial * per_column, LANES), jnp.float32),
            jax.ShapeDtypeStruct((edge + 8, LANES), jnp.float32),
            jax.ShapeDtypeStruct((edge + 8, LANES), jnp.float32),
        ),
        in_specs=smem(2) + [pl.BlockSpec(memory_space=pl.ANY)] * 2,
        out_specs=tuple(vmem(3)),
        scratch_shapes=[pltpu.VMEM(block, jnp.float32), pltpu.SemaphoreType.DMA((FIELDS,))],
        compiler_params=params(),
        name="pack",
    )(shifts, fractions, density, velocity)
    below = lax.ppermute(right, "row", [(i, i + 1) for i in range(bands - 1)])
    above = lax.ppermute(left, "row", [(i + 1, i) for i in range(bands - 1)])
    ext_shift = jnp.concatenate([below[edge, :1].astype(jnp.int32), shifts, above[edge, :1].astype(jnp.int32)])
    ext_frac = jnp.concatenate([below[edge + 1, :1], fractions, above[edge + 1, :1]])

    cuts = [columns * p // PARTS for p in range(PARTS + 1)] if columns % (PARTS * INNER) == 0 else [0, columns]
    spans = list(zip(cuts[:-1], cuts[1:]))
    sent = [(low + 2 * HALO if low else 0, high + 2 * HALO) for low, high in spans]
    chunks = pl.pallas_call(
        functools.partial(chunk_kernel, cycle, sent),
        out_shape=[jax.ShapeDtypeStruct(((high - low) * per_column, LANES), jnp.float32) for low, high in sent for _ in range(cycle)],
        in_specs=smem(1) + vmem(3),
        out_specs=vmem(len(spans) * cycle),
        compiler_params=params(),
        name="chunk",
    )(where, rows, below, above)
    theta = (np.arange(polar) + 0.5) / polar
    tilt = (1.0 + 0.5 * np.cos(np.pi * theta)).reshape(INNER, groups).T
    tilt = jnp.asarray(np.tile(tilt, (1, LANES // INNER)), jnp.float32)

    rings = [exchange(chunks[p * cycle:(p + 1) * cycle], "phi") for p in range(len(spans))]
    back = []
    lights = []
    for p, (low, high) in enumerate(spans):
        width = high - low
        swap = cycle == INNER and width % INNER == 0
        segments = []
        taken = []
        for index, (begin, end) in enumerate(sent):
            begin_here, end_here = max(begin, low), min(end, high + 2 * HALO)
            if begin_here < end_here:
                segments.append((begin_here - low, end_here - low, (begin_here - begin) * per_column))
                taken += rings[index]
        chunk = jax.ShapeDtypeStruct((width * per_column, LANES), jnp.float32)
        slots = -(-width // INNER)
        wide = (width + 2 * HALO) * per_column * cycle
        *out, light = pl.pallas_call(
            functools.partial(evolve_kernel, cells, cycle, low, width, nrad, groups, segments),
            out_shape=[chunk] * cycle + [jax.ShapeDtypeStruct((width, LANES) if swap else (slots, cycle, LANES), jnp.float32)],
            in_specs=smem(3) + vmem(1 + len(taken)),
            out_specs=vmem(cycle + 1),
            scratch_shapes=[
                pltpu.VMEM((wide, LANES), jnp.float32),
                pltpu.VMEM((wide, LANES), jnp.float32),
                pltpu.VMEM((width * per_column * cycle, LANES), jnp.float32),
            ],
            compiler_params=params(),
            name="evolve",
        )(ext_shift, ext_frac, where, tilt, *taken)
        if not swap:
            light = light.reshape(slots, cycle, cells, INNER).transpose(0, 3, 2, 1).reshape(slots * INNER, nphi)[:width]
        lights.append(light)
        back += exchange(out, "phi")

    light = jnp.concatenate(lights)
    if columns % 8 == 0:
        pieces = exchange([light] * cycle, "phi")
        table = pl.pallas_call(
            functools.partial(gather_kernel, cycle),
            out_shape=jax.ShapeDtypeStruct((radial, nphi), jnp.float32),
            in_specs=smem(1) + vmem(cycle),
            out_specs=pl.BlockSpec(memory_space=pltpu.VMEM),
            compiler_params=params(),
            name="gather",
        )(where, *pieces)
    else:
        table = lax.all_gather(light, "phi", axis=0, tiled=True)
    table = lax.all_gather(table, "row", axis=0, tiled=True)

    density_out, velocity_out = pl.pallas_call(
        functools.partial(unpack_kernel, cycle, spans),
        out_shape=(
            jax.ShapeDtypeStruct(density.shape, jnp.float32),
            jax.ShapeDtypeStruct(velocity.shape, jnp.float32),
        ),
        in_specs=smem(1) + vmem(len(back)),
        out_specs=[pl.BlockSpec(memory_space=pl.ANY)] * 2,
        scratch_shapes=[
            pltpu.VMEM((radial * per_column, LANES), jnp.float32),
            pltpu.VMEM(block, jnp.float32),
            pltpu.SemaphoreType.DMA((FIELDS,)),
        ],
        compiler_params=params(),
        name="unpack",
    )(where, *back)

    rows_dev = NPIX // (cycle * bands)
    first_row = (place * bands + row) * rows_dev
    geometry = pixel_tiles(first_row, rows_dev, NPIX, nphi, nrad)
    image = draw_image(table, geometry, cells, cycle, rows_dev, NPIX, nphi, nrad)
    return (density_out, velocity_out, image)


def solution(mesh):
    in_specs = (P("phi", None, "row"), P(None, "phi", None, "row"), P("row"), P("row"))
    out_specs = (P("phi", None, "row"), P(None, "phi", None, "row"), P(("phi", "row"), None))
    return jax.shard_map(body, mesh=mesh, in_specs=in_specs, out_specs=out_specs, check_vma=False)
```

```python
import functools

import jax
import jax.numpy as jnp
import numpy as np
from jax import lax
from jax.experimental import pallas as pl
from jax.experimental.pallas import tpu as pltpu
from jax.sharding import PartitionSpec as P

BAND = 8
STEPS = 2
NPIX = 1024


SPEED = 1.5
COURANT = 0.05
KAPPA = 1.5
R_INNER = 0.2

FIELDS = 4
INNER = 8
HALO = STEPS
LANES = 128
VMEM_LIMIT = 48 * 1024 * 1024
PACK_LIMIT = 62 * 1024 * 1024


def params():
    return pltpu.CompilerParams(vmem_limit_bytes=VMEM_LIMIT)


def vmem(count):
    return [pl.BlockSpec(memory_space=pltpu.VMEM)] * count


def smem(count):
    return [pl.BlockSpec(memory_space=pltpu.SMEM)] * count


def field_ref(density_ref, velocity_ref, field):
    return density_ref if field == 0 else velocity_ref.at[field - 1]


def pack_kernel(density_ref, velocity_ref, *refs):
    *chunk_refs, rows_ref, field_refs, arrived = refs
    cells, polar, radial = density_ref.shape
    groups = polar // INNER
    per_column = FIELDS * groups
    stride = radial // len(chunk_refs) * per_column
    place = lax.axis_index("phi")
    copies = [
        pltpu.make_async_copy(field_ref(density_ref, velocity_ref, field), field_refs.at[field], arrived.at[field])
        for field in range(FIELDS)
    ]
    for copy in copies:
        copy.start()
    for field in range(FIELDS):
        copies[field].wait()
        for group in range(groups):
            block = field_refs[field, :, pl.ds(group, INNER, stride=groups), :]
            turned = block.reshape(cells * INNER, radial).T
            rows_ref[pl.ds(field * groups + group, radial, stride=per_column), :] = turned
    for j, chunk_ref in enumerate(chunk_refs):
        chunk_ref[...] = rows_ref[pl.ds(pl.multiple_of(partner(place, j, len(chunk_refs)) * stride, stride), stride), :]


def halo_kernel(cycle, columns, shift_ref, frac_ref, *refs):
    chunk_refs, piece_refs = refs[:cycle], refs[cycle:]
    rows = chunk_refs[0].shape[0]
    edge = HALO * rows // columns
    place = lax.axis_index("phi")
    sub = lax.broadcasted_iota(jnp.int32, (8, LANES), 0)
    odd = place % 2
    for ref, upper in zip(piece_refs, (odd == 0, odd == 1)):
        at = pl.multiple_of(jnp.where(upper, rows - edge, 0), 8)
        for j in range(cycle):
            ref[pl.ds(partner(place, j, cycle), edge, stride=cycle), :] = chunk_refs[j][pl.ds(at, edge), :]
        band = (place * columns + jnp.where(upper, columns - 1, 0)) // BAND
        ref[pl.ds(edge * cycle, 8), :] = jnp.where(sub == 0, shift_ref[band].astype(jnp.float32), frac_ref[band])


def unpack_kernel(cycle, cuts, *refs):
    *chunk_refs, density_ref, velocity_ref, rows_ref, field_refs, leaving = refs
    first_refs, rest_refs = chunk_refs[:cycle], chunk_refs[cycle:]
    cells, polar, radial = density_ref.shape
    groups = polar // INNER
    per_column = FIELDS * groups
    stride = radial // cycle * per_column
    place = lax.axis_index("phi")
    rest = iter(rest_refs)
    for j, cut in enumerate(cuts):
        at = partner(place, j, cycle) * stride
        rows_ref[pl.ds(pl.multiple_of(at, per_column), cut), :] = first_refs[j][pl.ds(0, cut), :]
        if cut < stride:
            rows_ref[pl.ds(pl.multiple_of(at + cut, per_column), stride - cut), :] = next(rest)[...]
    copies = []
    for field in range(FIELDS):
        for group in range(groups):
            turned = rows_ref[pl.ds(field * groups + group, radial, stride=per_column), :]
            block = turned.T.reshape(cells, INNER, radial)
            field_refs[field, :, pl.ds(group, INNER, stride=groups), :] = block
        copy = pltpu.make_async_copy(field_refs.at[field], field_ref(density_ref, velocity_ref, field), leaving.at[field])
        copy.start()
        copies.append(copy)
    for copy in copies:
        copy.wait()


def stepper(cells, cycle, columns, nrad, groups, band_of):
    first_global = (lax.axis_index("row") * cycle + lax.axis_index("phi")) * columns
    lane = lax.broadcasted_iota(jnp.int32, (cycle, LANES), 1)
    inner = lane % INNER

    def upper_azimuth(x):
        z = pltpu.roll(x, LANES - INNER, 1)
        return jnp.where(lane < LANES - INNER, z, pltpu.roll(z, cycle - 1, 0))

    def lower_azimuth(x):
        z = pltpu.roll(x, INNER, 1)
        return jnp.where(lane >= INNER, z, pltpu.roll(z, 1, 0))

    def upper_polar(x):
        last = jnp.where(inner == INNER - 1, 0.0, pltpu.roll(x[0], LANES - 1, 1))
        return x[1:] + [last]

    def lower_polar(x):
        head = jnp.where(inner == 0, 0.0, pltpu.roll(x[-1], 1, 1))
        return [head] + x[:-1]

    def conserved(prim):
        return [prim[0]] + [[r * v for r, v in zip(prim[0], prim[k])] for k in (1, 2, 3)]

    half = 0.5 * COURANT
    damp = 0.5 * SPEED * COURANT

    def face_part(cons, speed, comp, sign):
        factor = [half * u + sign * damp for u in speed]
        parts = [[c * m for c, m in zip(cons[k], factor)] for k in range(FIELDS)]
        parts[comp] = [p + half * r for p, r in zip(parts[comp], cons[0])]
        return parts

    def contributions(prim):
        cons = conserved(prim)
        a_phi = face_part(cons, prim[2], 2, -1.0)
        b_phi = face_part(cons, prim[2], 2, 1.0)
        a_th = face_part(cons, prim[3], 3, -1.0)
        b_th = face_part(cons, prim[3], 3, 1.0)
        keep = 1.0 - 3.0 * SPEED * COURANT
        pend = []
        for k in range(FIELDS):
            up_t = upper_polar(a_th[k])
            low_t = lower_polar(b_th[k])
            pend.append([
                keep * cons[k][g] - (upper_azimuth(a_phi[k][g]) - lower_azimuth(b_phi[k][g])) - (up_t[g] - low_t[g])
                for g in range(groups)
            ])
        return pend, face_part(cons, prim[1], 1, -1.0), face_part(cons, prim[1], 1, 1.0)

    def combine(x, y, sign):
        return [[p + q if sign > 0 else p - q for p, q in zip(a, b)] for a, b in zip(x, y)]

    def finish(fresh, col):
        number = first_global + col - HALO
        valid = (number >= 0) & (number < nrad)
        shift, weight = band_of(col)
        turn = shift // cells
        step = INNER * (shift % cells)
        inside = lane >= step
        inverse = [1.0 / r for r in fresh[0]]
        prim = [fresh[0]] + [[m * i for m, i in zip(fresh[k], inverse)] for k in (1, 2, 3)]
        moved = []
        for k in range(FIELDS):
            row = []
            for x in prim[k]:
                x = jnp.where(valid, x, 0.0)
                x = (1.0 - weight) * x + weight * lower_azimuth(x)
                z = pltpu.roll(x, step, 1)
                z = jnp.where(inside, z, pltpu.roll(z, 1, 0))
                row.append(pltpu.roll(z, turn, 0))
            moved.append(row)
        return moved

    def step_columns(read, write, low, high):
        prim = read(low)
        before = face_part(conserved(prim), prim[1], 1, 1.0)
        pend, _, after = contributions(read(low + 1))
        pend = combine(pend, before, 1.0)

        def body(col, carry):
            pend, before = carry
            fresh_pend, a_rad, b_rad = contributions(read(col))
            write(col - 1, finish(combine(pend, a_rad, -1.0), col - 1))
            return combine(fresh_pend, before, 1.0), b_rad

        pend, _ = lax.fori_loop(low + 2, high - 1, body, (pend, after), unroll=4)
        prim = read(high - 1)
        a_rad = face_part(conserved(prim), prim[1], 1, -1.0)
        write(high - 2, finish(combine(pend, a_rad, -1.0), high - 2))

    return step_columns


def block_rows(cycle, groups):
    def at(col, k, g):
        return pl.ds(pl.multiple_of(((col * FIELDS + k) * groups + g) * cycle, cycle), cycle)

    def reader(ref, first=0):
        return lambda col: [[ref[at(col - first, k, g), :] for g in range(groups)] for k in range(FIELDS)]

    def writer(ref, first=0):
        def write(col, prim):
            for k in range(FIELDS):
                for g in range(groups):
                    ref[at(col - first, k, g), :] = prim[k][g]

        return write

    return at, reader, writer


def inner_kernel(cells, cycle, columns, nrad, groups, shift_ref, frac_ref, *refs):
    chunk_refs, (work_ref, own_ref) = refs[:cycle], refs[cycle:]
    per_column = FIELDS * groups
    _, reader, writer = block_rows(cycle, groups)
    place = lax.axis_index("phi")
    for j in range(cycle):
        own_ref[pl.ds(partner(place, j, cycle), columns * per_column, stride=cycle), :] = chunk_refs[j][...]

    def band_of(col):
        band = (place * columns + col - HALO) // BAND
        return shift_ref[band], frac_ref[band]

    step_columns = stepper(cells, cycle, columns, nrad, groups, band_of)
    if columns > 2:
        step_columns(reader(own_ref, HALO), writer(work_ref, HALO + 1), HALO, HALO + columns)


def outer_kernel(cells, cycle, columns, nrad, groups, cuts, shift_ref, frac_ref, tilt_ref, first_ref, second_ref, inner_ref, *refs):
    chunk_refs, refs = refs[:cycle], refs[cycle:]
    *out_refs, strip_ref, work_ref, done_ref = refs
    first_refs, rest_refs = out_refs[:cycle], out_refs[cycle:]
    swap = first_refs[0].shape[0] > cuts[0]
    per_column = FIELDS * groups
    edge = HALO * per_column * cycle
    at, reader, writer = block_rows(cycle, groups)
    place = lax.axis_index("phi")
    first_global = (lax.axis_index("row") * cycle + place) * columns

    odd = place % 2 == 1

    def carried(rows):
        return rows.astype(jnp.int32)[0, 0], rows[1, 0]

    tails = [ref[pl.ds(edge, 8), :] for ref in (first_ref, second_ref)]
    below = carried(jnp.where(odd, tails[0], tails[1]))
    above = carried(jnp.where(odd, tails[1], tails[0]))

    def band_of(col):
        band = jnp.clip((place * columns + col - HALO) // BAND, 0, shift_ref.shape[0] - 1)
        low, high = col < HALO, col >= HALO + columns
        shift = jnp.where(low, below[0], jnp.where(high, above[0], shift_ref[band]))
        weight = jnp.where(low, below[1], jnp.where(high, above[1], frac_ref[band]))
        return shift, weight

    step_columns = stepper(cells, cycle, columns, nrad, groups, band_of)
    strip_ref[pl.ds(pl.multiple_of(jnp.where(odd, 0, 3 * edge), 8), edge), :] = first_ref[pl.ds(0, edge), :]
    strip_ref[pl.ds(pl.multiple_of(jnp.where(odd, 3 * edge, 0), 8), edge), :] = second_ref[pl.ds(0, edge), :]
    rows = columns * per_column
    for j in range(cycle):
        slab = partner(place, j, cycle)
        strip_ref[pl.ds(edge + slab, edge // cycle, stride=cycle), :] = chunk_refs[j][pl.ds(0, edge // cycle), :]
        strip_ref[pl.ds(2 * edge + slab, edge // cycle, stride=cycle), :] = chunk_refs[j][pl.ds(rows - edge // cycle, edge // cycle), :]
    kept = (columns - 2) * per_column * cycle
    if kept:
        work_ref[pl.ds((HALO + 1) * per_column * cycle, kept), :] = inner_ref[pl.ds(0, kept), :]
    step_columns(reader(strip_ref), writer(work_ref), 0, 2 * HALO)
    step_columns(reader(strip_ref, columns - 2 * HALO), writer(work_ref), columns, columns + 2 * HALO)
    step_columns(reader(work_ref), writer(done_ref, HALO), 1, columns + 2 * HALO - 1)
    rest = iter(rest_refs)
    for j, cut in enumerate(cuts):
        slab = partner(place, j, cycle)
        first_refs[j][pl.ds(0, cut), :] = done_ref[pl.ds(slab, cut, stride=cycle), :]
        if cut < rows:
            next(rest)[...] = done_ref[pl.ds(cut * cycle + slab, rows - cut, stride=cycle), :]
    lane = lax.broadcasted_iota(jnp.int32, (cycle, LANES), 1)
    inner = lane % INNER

    def column_light(own):
        dtau = [(KAPPA / (groups * INNER)) * done_ref[at(own, 0, g), :] for g in range(groups)]
        total = dtau[0]
        for d in dtau[1:]:
            total = total + d
        run = total
        for d in (1, 2, 4):
            run = run + jnp.where(inner >= d, pltpu.roll(run, d, 1), 0.0)
        above = run - total
        light = jnp.zeros_like(total)
        for g in range(groups):
            light = light + tilt_ref[pl.ds(g, 1), :] * (1.0 - jnp.exp(-dtau[g])) * jnp.exp(-above)
            above = above + dtau[g]
        for d in (1, 2, 4):
            light = light + pltpu.roll(light, LANES - d, 1)
        number = jnp.full((cycle, LANES), first_global + own, jnp.int32).astype(jnp.float32)
        radius = R_INNER + (number + 0.5) * (1.0 - R_INNER) / nrad
        return pltpu.roll(light * (1.0 / jnp.sqrt(radius)), own % INNER, 1)

    for h in range(-(-columns // INNER)):
        slots = range(min(INNER, columns - h * INNER))
        x = jnp.zeros((cycle, LANES), jnp.float32)
        for slot, light in [(slot, column_light(h * INNER + slot)) for slot in slots]:
            x = jnp.where(inner == slot, light, x)
        if swap:
            sub = lax.broadcasted_iota(jnp.int32, (cycle, LANES), 0)
            for d in (1, 2, 4):
                low_sub = (sub & d) == 0
                low_lane = (lane & d) == 0
                ahead = pltpu.roll(pltpu.roll(x, cycle - d, 0), d, 1)
                back = pltpu.roll(pltpu.roll(x, d, 0), LANES - d, 1)
                x = jnp.where(low_sub == low_lane, x, jnp.where(low_sub, ahead, back))
            for ref, cut in zip(first_refs, cuts):
                ref[pl.ds(cut + h * INNER, INNER), :] = x
        else:
            rest_refs[0][h] = x


def pixel_tiles(first_row, rows_dev, npix, nphi, nrad):
    tile_rows = min(8, rows_dev)
    tile_cols = LANES // tile_rows
    across = npix // tile_cols
    tiles = rows_dev // tile_rows * across
    tile = lax.broadcasted_iota(jnp.int32, (tiles, LANES), 0)
    pixel = lax.broadcasted_iota(jnp.int32, (tiles, LANES), 1)
    row = first_row + tile // across * tile_rows + pixel // tile_cols
    col = tile % across * tile_cols + pixel % tile_cols
    yy = (row.astype(jnp.float32) + 0.5) / npix * 2.0 - 1.0
    xx = (col.astype(jnp.float32) + 0.5) / npix * 2.0 - 1.0
    dist = jnp.sqrt(xx * xx + yy * yy)
    upos = (dist - R_INNER) / (1.0 - R_INNER) * nrad - 0.5
    floor_u = jnp.floor(upos)
    frac_u = upos - floor_u
    lower = jnp.clip(floor_u.astype(jnp.int32), -2, nrad) + LANES
    angle = jnp.arctan2(yy, xx)
    vpos = (angle + jnp.pi) / (2.0 * jnp.pi) * nphi - 0.5
    window = jnp.min(lower, axis=1) // (LANES // 2)
    window = jnp.clip(window, 0, (nrad + LANES) // (LANES // 2))
    start = jnp.clip(jnp.floor(jnp.min(vpos, axis=1)).astype(jnp.int32) + 8, 0, nphi + 8)
    spot = jnp.clip(lower - window[:, None] * (LANES // 2), 0, LANES - 2)
    return start, window, spot, frac_u, vpos + 8.0 - start[:, None].astype(jnp.float32)


def window_rows(rows_dev, npix, nphi):
    tile_rows = min(8, rows_dev)
    tile_cols = LANES // tile_rows
    diagonal = 2.0 * np.hypot(tile_rows, tile_cols) / npix
    span = diagonal / (R_INNER - diagonal) / (2.0 * np.pi) * nphi
    return -(-int(np.ceil(span) + 2) // 8) * 8


def image_kernel(cells, cycle, nphi, nrad, rows, tile_rows, across, start_ref, window_ref, spot_ref, frac_ref, vpos_ref, *refs):
    *table_refs, out_ref, turned_ref, wide_ref = refs
    blocks = nrad // LANES
    each = blocks // len(table_refs)
    for j, table_ref in enumerate(table_refs):
        for k in range(each):
            block = partner(lax.axis_index("row"), j, len(table_refs)) * each + k
            for l in range(nphi // LANES):
                at = pl.multiple_of(block * nphi + l * LANES, LANES)
                turned_ref[pl.ds(at, LANES), :] = table_ref[pl.ds(k * LANES, LANES), pl.ds(l * LANES, LANES)].T
    half = LANES // 2
    windows = 2 * (blocks + 2) - 1
    tall = wide_ref.shape[0] // windows

    def fill(s, carry):
        zero = jnp.zeros((cells, LANES), jnp.float32)
        value = [zero] + [turned_ref[pl.ds(k * nphi + s, cells, stride=cycle), :] for k in range(blocks)] + [zero]
        for w in range(windows):
            piece = value[w // 2]
            if w % 2:
                piece = jnp.concatenate([piece[:, half:], value[w // 2 + 1][:, :half]], axis=1)
            wide_ref[pl.ds((8 + s * cells) * windows + w, cells, stride=windows), :] = piece
        return carry

    lax.fori_loop(0, cycle, fill, 0, unroll=8)
    pad = tall - nphi - 8
    wide_ref[pl.ds(0, 8 * windows), :] = wide_ref[pl.ds(nphi * windows, 8 * windows), :]
    wide_ref[pl.ds((nphi + 8) * windows, pad * windows), :] = wide_ref[pl.ds(8 * windows, pad * windows), :]

    sub = lax.broadcasted_iota(jnp.int32, (8, LANES), 0)
    lane = lax.broadcasted_iota(jnp.int32, (8, LANES), 1)

    def one_tile(tile):
        start = start_ref[tile]
        at = start * windows + window_ref[tile]
        spot = jnp.broadcast_to(spot_ref[pl.ds(tile, 1), :], (8, LANES))
        frac = jnp.broadcast_to(frac_ref[pl.ds(tile, 1), :], (8, LANES))
        vpos = jnp.broadcast_to(vpos_ref[pl.ds(tile, 1), :], (8, LANES))
        total = None
        for r in range(0, rows, 8):
            block = wide_ref[pl.ds(at + r * windows, 8, stride=windows), :]
            low = jnp.take_along_axis(block, spot, axis=1)
            high = jnp.take_along_axis(block, spot + 1, axis=1)
            weight = jnp.maximum(0.0, 1.0 - jnp.abs((sub + r).astype(jnp.float32) - vpos))
            part = weight * (low + frac * (high - low))
            total = part if total is None else total + part
        return total

    def group(index, carry):
        parts = [one_tile(index * 8 + t) for t in range(8)]
        for d in (4, 2, 1):
            upper = (sub & d) != 0
            parts = [
                jnp.where(upper, b, a) + jnp.where(upper, pltpu.roll(b, d, 0), pltpu.roll(a, 8 - d, 0))
                for a, b in zip(parts[:d], parts[d:])
            ]
        result = parts[0]
        if tile_rows == 8:
            width = LANES // 8
            for d in (1, 2, 4):
                low_sub = (sub & d) == 0
                low_lane = (lane & (d * width)) == 0
                ahead = pltpu.roll(pltpu.roll(result, 8 - d, 0), d * width, 1)
                back = pltpu.roll(pltpu.roll(result, d, 0), LANES - d * width, 1)
                result = jnp.where(low_sub == low_lane, result, jnp.where(low_sub, ahead, back))
            per_row = across // 8
            out_ref[pl.ds(pl.multiple_of(index // per_row * 8, 8), 8), pl.ds(pl.multiple_of(index % per_row * LANES, LANES), LANES)] = result
        else:
            out_ref[pl.ds(pl.multiple_of(index * 8, 8), 8), :] = result
        return carry

    lax.fori_loop(0, spot_ref.shape[0] // 8, group, 0, unroll=min(8, spot_ref.shape[0] // 8))


def draw_image(tables, geometry, cells, cycle, rows_dev, npix, nphi, nrad):
    start, window, spot, frac_u, vpos = geometry
    tiles = spot.shape[0]
    tile_rows = min(8, rows_dev)
    tile_cols = LANES // tile_rows
    across = npix // tile_cols
    rows = window_rows(rows_dev, npix, nphi)
    windows = 2 * (nrad // LANES + 2) - 1
    shape = (rows_dev, npix) if tile_rows == 8 else (tiles, LANES)
    image = pl.pallas_call(
        functools.partial(image_kernel, cells, cycle, nphi, nrad, rows, tile_rows, across),
        out_shape=jax.ShapeDtypeStruct(shape, jnp.float32),
        in_specs=smem(2) + vmem(3 + len(tables)),
        out_specs=pl.BlockSpec(memory_space=pltpu.VMEM),
        scratch_shapes=[
            pltpu.VMEM((nphi * (nrad // LANES), LANES), jnp.float32),
            pltpu.VMEM(((nphi + 16 + rows) * windows, LANES), jnp.float32),
        ],
        compiler_params=params(),
        name="image",
    )(start, window, spot, frac_u, vpos, *tables)
    if tile_rows == 8:
        return image
    image = image.reshape(rows_dev // tile_rows, across, tile_rows, tile_cols)
    return jnp.swapaxes(image, 1, 2).reshape(rows_dev, npix)


def partner(place, index, size):
    return place ^ ((size - index) % size)


def swapped(piece, axis, index):
    size = lax.axis_size(axis)
    return lax.ppermute(piece, axis, [(p, partner(p, index, size)) for p in range(size)])


def exchange(chunks, axis):
    size = lax.axis_size(axis)
    if size > INNER:
        place, every = lax.axis_index(axis), jnp.arange(size)
        sent = jnp.stack(chunks)[(size - (place ^ every)) % size]
        got = lax.all_to_all(sent, axis, 0, 0, tiled=True)[partner(place, every, size)]
        return [got[i] for i in range(size)]
    return [chunks[0]] + [swapped(chunks[i], axis, i) for i in range(1, size)]


def gather_kernel(cuts, *refs):
    *piece_refs, out_ref = refs
    size = len(cuts)
    count = out_ref.shape[0] // size
    for j, cut in enumerate(cuts):
        out_ref[pl.ds(pl.multiple_of(partner(lax.axis_index("phi"), j, size) * count, count), count), :] = piece_refs[j][pl.ds(cut, count), :]


def neighbour_columns(first, second):
    cycle, bands = lax.axis_size("phi"), lax.axis_size("row")
    order = [q * bands + r for r in range(bands) for q in range(cycle)]
    pairs = list(zip(order[:-1], order[1:]))

    def both_ways(piece, chosen):
        return lax.ppermute(piece, ("phi", "row"), chosen + [(j, i) for i, j in chosen])

    return both_ways(first, pairs[::2]), both_ways(second, pairs[1::2])


def body(density, velocity, shifts, fractions):
    cycle = lax.axis_size("phi")
    bands = lax.axis_size("row")
    cells, polar, radial = density.shape
    groups = polar // INNER
    per_column = FIELDS * groups
    columns = radial // cycle
    nphi = cells * cycle
    nrad = radial * bands
    place = lax.axis_index("phi")
    row = lax.axis_index("row")
    block = (FIELDS, cells, polar, radial)
    hbm = pl.BlockSpec(memory_space=pltpu.HBM)

    def f32(*shape):
        return jax.ShapeDtypeStruct(shape, jnp.float32)

    chunk = f32(columns * per_column, LANES)
    chunks = pl.pallas_call(
        pack_kernel,
        out_shape=[chunk] * cycle,
        in_specs=[hbm] * 2,
        out_specs=vmem(cycle),
        scratch_shapes=[
            pltpu.VMEM((radial * per_column, LANES), jnp.float32),
            pltpu.VMEM(block, jnp.float32),
            pltpu.SemaphoreType.DMA((FIELDS,)),
        ],
        compiler_params=pltpu.CompilerParams(vmem_limit_bytes=PACK_LIMIT),
        name="pack",
    )(density, velocity)
    ring = exchange(chunks, "phi")

    column_rows = per_column * cycle
    edge = HALO * column_rows
    pieces = pl.pallas_call(
        functools.partial(halo_kernel, cycle, columns),
        out_shape=[f32(edge + 8, LANES)] * 2,
        in_specs=smem(2) + vmem(cycle),
        out_specs=vmem(2),
        compiler_params=params(),
        name="halo",
    )(shifts, fractions, *ring)
    first, second = neighbour_columns(*pieces)
    inner = pl.pallas_call(
        functools.partial(inner_kernel, cells, cycle, columns, nrad, groups),
        out_shape=f32(max(columns - 2, 1) * column_rows, LANES),
        in_specs=smem(2) + vmem(cycle),
        out_specs=pl.BlockSpec(memory_space=pltpu.VMEM),
        scratch_shapes=[pltpu.VMEM((columns * column_rows, LANES), jnp.float32)],
        compiler_params=params(),
        name="inner",
    )(shifts, fractions, *ring)
    theta = (np.arange(polar) + 0.5) / polar
    tilt = (1.0 + 0.5 * np.cos(np.pi * theta)).reshape(INNER, groups).T
    tilt = jnp.asarray(np.tile(tilt, (1, LANES // INNER)), jnp.float32)
    swap = cycle == INNER and columns % INNER == 0
    rows = columns * per_column
    cuts = [rows] * cycle
    if swap:
        for j in range(1, cycle // 2 + 1):
            cuts[j] = columns // 2 * per_column
        extra = [f32(rows - cut, LANES) for cut in cuts if cut < rows]
    else:
        slots = -(-columns // INNER)
        extra = [f32(slots, cycle, LANES)]
    out = pl.pallas_call(
        functools.partial(outer_kernel, cells, cycle, columns, nrad, groups, cuts),
        out_shape=[f32(cut + (columns if swap else 0), LANES) for cut in cuts] + extra,
        in_specs=smem(2) + vmem(4 + cycle),
        out_specs=vmem(cycle + len(extra)),
        scratch_shapes=[
            pltpu.VMEM((4 * edge, LANES), jnp.float32),
            pltpu.VMEM(((columns + 2 * HALO) * column_rows, LANES), jnp.float32),
            pltpu.VMEM((columns * column_rows, LANES), jnp.float32),
        ],
        compiler_params=params(),
        name="outer",
    )(shifts, fractions, tilt, first, second, inner, *ring)
    back = exchange(out[:cycle], "phi")
    if swap:
        table = pl.pallas_call(
            functools.partial(gather_kernel, cuts),
            out_shape=f32(radial, nphi),
            in_specs=vmem(cycle),
            out_specs=pl.BlockSpec(memory_space=pltpu.VMEM),
            compiler_params=params(),
            name="gather",
        )(*back)
        back += [
            swapped(piece, "phi", j) for piece, j in zip(out[cycle:], [j for j in range(cycle) if cuts[j] < rows])
        ]
    else:
        light = out[cycle].reshape(slots, cycle, cells, INNER).transpose(0, 3, 2, 1).reshape(slots * INNER, nphi)[:columns]
        table = lax.all_gather(light, "phi", axis=0, tiled=True)
    tables = exchange([table] * bands, "row")

    rows_dev = NPIX // (cycle * bands)
    first_row = (place * bands + row) * rows_dev
    geometry = pixel_tiles(first_row, rows_dev, NPIX, nphi, nrad)
    image = draw_image(tables, geometry, cells, cycle, rows_dev, NPIX, nphi, nrad)
    density_out, velocity_out = pl.pallas_call(
        functools.partial(unpack_kernel, cycle, cuts),
        out_shape=(f32(*density.shape), f32(*velocity.shape)),
        in_specs=vmem(len(back)),
        out_specs=[hbm] * 2,
        scratch_shapes=[
            pltpu.VMEM((radial * per_column, LANES), jnp.float32),
            pltpu.VMEM(block, jnp.float32),
            pltpu.SemaphoreType.DMA((FIELDS,)),
        ],
        compiler_params=params(),
        name="unpack",
    )(*back)

    return (density_out, velocity_out, image)


def solution(mesh):
    in_specs = (P("phi", None, "row"), P(None, "phi", None, "row"), P("row"), P("row"))
    out_specs = (P("phi", None, "row"), P(None, "phi", None, "row"), P(("phi", "row"), None))
    return jax.shard_map(body, mesh=mesh, in_specs=in_specs, out_specs=out_specs, check_vma=False)
```

```python
import functools

import jax
import jax.numpy as jnp
import numpy as np
from jax import lax
from jax.experimental import pallas as pl
from jax.experimental.pallas import tpu as pltpu
from jax.sharding import PartitionSpec as P

BAND = 8
STEPS = 2
NPIX = 1024


SPEED = 1.5
COURANT = 0.05
KAPPA = 1.5
R_INNER = 0.2

FIELDS = 4
INNER = 8
HALO = STEPS
LANES = 128
SPLIT = 1
ORDER = (0, 7, 1, 6, 2, 5, 3, 4)
VMEM_LIMIT = 48 * 1024 * 1024
PACK_LIMIT = 62 * 1024 * 1024


def params():
    return pltpu.CompilerParams(vmem_limit_bytes=VMEM_LIMIT)


def vmem(count):
    return [pl.BlockSpec(memory_space=pltpu.VMEM)] * count


def smem(count):
    return [pl.BlockSpec(memory_space=pltpu.SMEM)] * count


def field_ref(density_ref, velocity_ref, field):
    return density_ref if field == 0 else velocity_ref.at[field - 1]


def pack_kernel(density_ref, velocity_ref, *refs):
    *chunk_refs, rows_ref, field_refs, arrived = refs
    cells, polar, radial = density_ref.shape
    groups = polar // INNER
    per_column = FIELDS * groups
    stride = radial // len(chunk_refs) * per_column
    place = lax.axis_index("phi")
    part = cells // SPLIT
    copies = [
        pltpu.make_async_copy(
            field_ref(density_ref, velocity_ref, field).at[pl.ds(h * part, part)],
            field_refs.at[field, pl.ds(h * part, part)],
            arrived.at[field * SPLIT + h],
        )
        for field in range(FIELDS)
        for h in range(SPLIT)
    ]
    for copy in copies:
        copy.start()
    for field in range(FIELDS):
        for copy in copies[field * SPLIT:(field + 1) * SPLIT]:
            copy.wait()
        for group in range(groups):
            block = field_refs[field, :, pl.ds(group, INNER, stride=groups), :]
            turned = block.reshape(cells * INNER, radial).T
            rows_ref[pl.ds(field * groups + group, radial, stride=per_column), :] = turned
    for j, chunk_ref in enumerate(chunk_refs):
        chunk_ref[...] = rows_ref[pl.ds(pl.multiple_of(partner(place, j, len(chunk_refs)) * stride, stride), stride), :]


def halo_kernel(cycle, columns, early, shift_ref, frac_ref, *refs):
    chunk_refs, piece_refs = refs[:cycle], refs[cycle + early:]
    rows = chunk_refs[0].shape[0]
    edge = HALO * rows // columns
    place = lax.axis_index("phi")
    sub = lax.broadcasted_iota(jnp.int32, (8, LANES), 0)
    odd = place % 2
    for ref, upper in zip(piece_refs, (odd == 0, odd == 1)):
        at = pl.multiple_of(jnp.where(upper, rows - edge, 0), 8)
        for j in range(cycle):
            ref[pl.ds(partner(place, j, cycle), edge, stride=cycle), :] = chunk_refs[j][pl.ds(at, edge), :]
        band = (place * columns + jnp.where(upper, columns - 1, 0)) // BAND
        ref[pl.ds(edge * cycle, 8), :] = jnp.where(sub == 0, shift_ref[band].astype(jnp.float32), frac_ref[band])


def unpack_kernel(*refs):
    *chunk_refs, density_ref, velocity_ref, rows_ref, field_refs, leaving = refs
    cells, polar, radial = density_ref.shape
    groups = polar // INNER
    per_column = FIELDS * groups
    stride = radial // len(chunk_refs) * per_column
    place = lax.axis_index("phi")
    for j, chunk_ref in enumerate(chunk_refs):
        at = pl.multiple_of(partner(place, j, len(chunk_refs)) * stride, stride)
        rows_ref[pl.ds(at, stride), :] = chunk_ref[pl.ds(0, stride), :]
    part = cells // SPLIT
    copies = []
    for field in range(FIELDS):
        for group in range(groups):
            turned = rows_ref[pl.ds(field * groups + group, radial, stride=per_column), :]
            block = turned.T.reshape(cells, INNER, radial)
            field_refs[field, :, pl.ds(group, INNER, stride=groups), :] = block
        for h in range(SPLIT):
            here = pl.ds(h * part, part)
            copy = pltpu.make_async_copy(
                field_refs.at[field, here], field_ref(density_ref, velocity_ref, field).at[here], leaving.at[field * SPLIT + h]
            )
            copy.start()
            copies.append(copy)
    for copy in copies:
        copy.wait()


def stepper(cells, cycle, columns, nrad, groups, band_of):
    first_global = (lax.axis_index("row") * cycle + lax.axis_index("phi")) * columns
    lane = lax.broadcasted_iota(jnp.int32, (cycle, LANES), 1)
    inner = lane % INNER

    def upper_azimuth(x):
        z = pltpu.roll(x, LANES - INNER, 1)
        return jnp.where(lane < LANES - INNER, z, pltpu.roll(z, cycle - 1, 0))

    def lower_azimuth(x):
        z = pltpu.roll(x, INNER, 1)
        return jnp.where(lane >= INNER, z, pltpu.roll(z, 1, 0))

    def upper_polar(x):
        last = jnp.where(inner == INNER - 1, 0.0, pltpu.roll(x[0], LANES - 1, 1))
        return x[1:] + [last]

    def lower_polar(x):
        head = jnp.where(inner == 0, 0.0, pltpu.roll(x[-1], 1, 1))
        return [head] + x[:-1]

    def conserved(prim):
        return [prim[0]] + [[r * v for r, v in zip(prim[0], prim[k])] for k in (1, 2, 3)]

    half = 0.5 * COURANT
    damp = 0.5 * SPEED * COURANT

    def face_part(cons, speed, comp, sign):
        factor = [half * u + sign * damp for u in speed]
        parts = [[c * m for c, m in zip(cons[k], factor)] for k in range(FIELDS)]
        parts[comp] = [p + half * r for p, r in zip(parts[comp], cons[0])]
        return parts

    def contributions(prim):
        cons = conserved(prim)
        a_phi = face_part(cons, prim[2], 2, -1.0)
        b_phi = face_part(cons, prim[2], 2, 1.0)
        a_th = face_part(cons, prim[3], 3, -1.0)
        b_th = face_part(cons, prim[3], 3, 1.0)
        keep = 1.0 - 3.0 * SPEED * COURANT
        pend = []
        for k in range(FIELDS):
            up_t = upper_polar(a_th[k])
            low_t = lower_polar(b_th[k])
            pend.append([
                keep * cons[k][g] - (upper_azimuth(a_phi[k][g]) - lower_azimuth(b_phi[k][g])) - (up_t[g] - low_t[g])
                for g in range(groups)
            ])
        return pend, face_part(cons, prim[1], 1, -1.0), face_part(cons, prim[1], 1, 1.0)

    def combine(x, y, sign):
        return [[p + q if sign > 0 else p - q for p, q in zip(a, b)] for a, b in zip(x, y)]

    def finish(fresh, col):
        number = first_global + col - HALO
        valid = (number >= 0) & (number < nrad)
        shift, weight = band_of(col)
        turn = shift // cells
        step = INNER * (shift % cells)
        inside = lane >= step
        inverse = [1.0 / r for r in fresh[0]]
        prim = [fresh[0]] + [[m * i for m, i in zip(fresh[k], inverse)] for k in (1, 2, 3)]
        moved = []
        for k in range(FIELDS):
            row = []
            for x in prim[k]:
                x = jnp.where(valid, x, 0.0)
                x = (1.0 - weight) * x + weight * lower_azimuth(x)
                z = pltpu.roll(x, step, 1)
                z = jnp.where(inside, z, pltpu.roll(z, 1, 0))
                row.append(pltpu.roll(z, turn, 0))
            moved.append(row)
        return moved

    def step_columns(read, write, low, high):
        prim = read(low)
        before = face_part(conserved(prim), prim[1], 1, 1.0)
        pend, _, after = contributions(read(low + 1))
        pend = combine(pend, before, 1.0)

        def body(col, carry):
            pend, before = carry
            fresh_pend, a_rad, b_rad = contributions(read(col))
            write(col - 1, finish(combine(pend, a_rad, -1.0), col - 1))
            return combine(fresh_pend, before, 1.0), b_rad

        carry = (pend, after)
        if high - low <= 8:
            for col in range(low + 2, high - 1):
                carry = body(col, carry)
        else:
            carry = lax.fori_loop(low + 2, high - 1, body, carry, unroll=4)
        pend = carry[0]
        prim = read(high - 1)
        a_rad = face_part(conserved(prim), prim[1], 1, -1.0)
        write(high - 2, finish(combine(pend, a_rad, -1.0), high - 2))

    return step_columns


def block_rows(cycle, groups):
    def at(col, k, g):
        return pl.ds(pl.multiple_of(((col * FIELDS + k) * groups + g) * cycle, cycle), cycle)

    def reader(ref, first=0):
        return lambda col: [[ref[at(col - first, k, g), :] for g in range(groups)] for k in range(FIELDS)]

    def writer(ref, first=0):
        def write(col, prim):
            for k in range(FIELDS):
                for g in range(groups):
                    ref[at(col - first, k, g), :] = prim[k][g]

        return write

    return at, reader, writer


def lit_columns(cycle, nrad, groups, first_global, tilt_ref, done_ref, cols, total_columns):
    at, _, _ = block_rows(cycle, groups)
    lane = lax.broadcasted_iota(jnp.int32, (cycle, LANES), 1)
    inner = lane % INNER

    def column_light(own):
        dtau = [(KAPPA / (groups * INNER)) * done_ref[at(own, 0, g), :] for g in range(groups)]
        total = dtau[0]
        for d in dtau[1:]:
            total = total + d
        run = total
        for d in (1, 2, 4):
            run = run + jnp.where(inner >= d, pltpu.roll(run, d, 1), 0.0)
        above = run - total
        light = jnp.zeros_like(total)
        for g in range(groups):
            light = light + tilt_ref[pl.ds(g, 1), :] * (1.0 - jnp.exp(-dtau[g])) * jnp.exp(-above)
            above = above + dtau[g]
        for d in (1, 2, 4):
            light = light + pltpu.roll(light, LANES - d, 1)
        number = jnp.full((cycle, LANES), first_global + own, jnp.int32).astype(jnp.float32)
        radius = R_INNER + (number + 0.5) * (1.0 - R_INNER) / nrad
        return pltpu.roll(light * (1.0 / jnp.sqrt(radius)), own % INNER, 1)

    blocks = []
    for h in range(-(-total_columns // INNER)):
        x = jnp.zeros((cycle, LANES), jnp.float32)
        for own, light in [(own, column_light(own)) for own in cols if own // INNER == h]:
            x = jnp.where(inner == own % INNER, light, x)
        blocks.append(x)
    return blocks


def inner_kernel(cells, cycle, columns, nrad, groups, margin, shift_ref, frac_ref, tilt_ref, *refs):
    chunk_refs, (done_ref, side_ref, light_ref, own_ref, work_ref) = refs[:cycle], refs[cycle:]
    per_column = FIELDS * groups
    side = HALO * per_column * cycle
    _, reader, writer = block_rows(cycle, groups)
    place = lax.axis_index("phi")
    for j in range(cycle):
        own_ref[pl.ds(partner(place, j, cycle), columns * per_column, stride=cycle), :] = chunk_refs[j][...]

    def band_of(col):
        band = (place * columns + col - HALO) // BAND
        return shift_ref[band], frac_ref[band]

    first_global = (lax.axis_index("row") * cycle + place) * columns
    step_columns = stepper(cells, cycle, columns, nrad, groups, band_of)
    last = HALO + columns
    step_columns(reader(own_ref, HALO), writer(work_ref, HALO), HALO, last)
    step_columns(reader(work_ref, HALO), writer(done_ref, HALO), HALO + 1, last - 1)
    one = side // HALO
    side_ref[pl.ds(0, side), :] = work_ref[pl.ds(one, side), :]
    side_ref[pl.ds(side, side), :] = work_ref[pl.ds((columns - 1) * one - side, side), :]
    blocks = lit_columns(cycle, nrad, groups, first_global, tilt_ref, done_ref, range(margin, columns - margin), columns)
    for h, x in enumerate(blocks):
        light_ref[h] = x


def outer_kernel(cells, cycle, columns, nrad, groups, margin, swap, shift_ref, frac_ref, tilt_ref, first_ref, second_ref, *refs):
    chunk_refs, refs = refs[:cycle], refs[cycle:]
    if margin:
        inner_ref, side_ref, lit_ref, *refs = refs
    *out_refs, strip_ref, work_ref, done_ref = refs
    out_refs, light_refs = out_refs[:cycle], out_refs[cycle:]
    per_column = FIELDS * groups
    column_rows = per_column * cycle
    edge = HALO * column_rows
    _, reader, writer = block_rows(cycle, groups)
    place = lax.axis_index("phi")
    first_global = (lax.axis_index("row") * cycle + place) * columns

    odd = place % 2 == 1

    def carried(rows):
        return rows.astype(jnp.int32)[0, 0], rows[1, 0]

    tails = [ref[pl.ds(edge, 8), :] for ref in (first_ref, second_ref)]
    below = carried(jnp.where(odd, tails[0], tails[1]))
    above = carried(jnp.where(odd, tails[1], tails[0]))

    def band_of(col):
        band = jnp.clip((place * columns + col - HALO) // BAND, 0, shift_ref.shape[0] - 1)
        low, high = col < HALO, col >= HALO + columns
        shift = jnp.where(low, below[0], jnp.where(high, above[0], shift_ref[band]))
        weight = jnp.where(low, below[1], jnp.where(high, above[1], frac_ref[band]))
        return shift, weight

    step_columns = stepper(cells, cycle, columns, nrad, groups, band_of)
    strip_ref[pl.ds(pl.multiple_of(jnp.where(odd, 0, 3 * edge), 8), edge), :] = first_ref[pl.ds(0, edge), :]
    strip_ref[pl.ds(pl.multiple_of(jnp.where(odd, 3 * edge, 0), 8), edge), :] = second_ref[pl.ds(0, edge), :]
    rows = columns * per_column
    for j in range(cycle):
        slab = partner(place, j, cycle)
        strip_ref[pl.ds(edge + slab, edge // cycle, stride=cycle), :] = chunk_refs[j][pl.ds(0, edge // cycle), :]
        strip_ref[pl.ds(2 * edge + slab, edge // cycle, stride=cycle), :] = chunk_refs[j][pl.ds(rows - edge // cycle, edge // cycle), :]
    step_columns(reader(strip_ref), writer(work_ref), 0, 2 * HALO)
    step_columns(reader(strip_ref, columns - 2 * HALO), writer(work_ref), columns, columns + 2 * HALO)
    if margin:
        work_ref[pl.ds((HALO + 1) * column_rows, edge), :] = side_ref[pl.ds(0, edge), :]
        work_ref[pl.ds((columns - 1) * column_rows, edge), :] = side_ref[pl.ds(edge, edge), :]
        kept = pl.ds(margin * column_rows, (columns - 2 * margin) * column_rows)
        done_ref[kept, :] = inner_ref[kept, :]
        step_columns(reader(work_ref), writer(done_ref, HALO), 1, 1 + 2 * HALO)
        step_columns(reader(work_ref), writer(done_ref, HALO), columns - 1, columns - 1 + 2 * HALO)
        cols = [*range(margin), *range(columns - margin, columns)]
    else:
        step_columns(reader(work_ref), writer(done_ref, HALO), 1, columns + 2 * HALO - 1)
        cols = range(columns)
    for j, out_ref in enumerate(out_refs):
        out_ref[pl.ds(0, rows), :] = done_ref[pl.ds(partner(place, j, cycle), rows, stride=cycle), :]
    lane = lax.broadcasted_iota(jnp.int32, (cycle, LANES), 1)
    for h, x in enumerate(lit_columns(cycle, nrad, groups, first_global, tilt_ref, done_ref, cols, columns)):
        if margin:
            x = x + lit_ref[h]
        if swap:
            sub = lax.broadcasted_iota(jnp.int32, (cycle, LANES), 0)
            for d in (1, 2, 4):
                low_sub = (sub & d) == 0
                low_lane = (lane & d) == 0
                ahead = pltpu.roll(pltpu.roll(x, cycle - d, 0), d, 1)
                back = pltpu.roll(pltpu.roll(x, d, 0), LANES - d, 1)
                x = jnp.where(low_sub == low_lane, x, jnp.where(low_sub, ahead, back))
            for out_ref in out_refs:
                out_ref[pl.ds(rows + h * INNER, INNER), :] = x
        else:
            light_refs[0][h] = x


def pixel_tiles(first_row, rows_dev, npix, nphi, nrad):
    tile_rows = min(8, rows_dev)
    tile_cols = LANES // tile_rows
    across = npix // tile_cols
    tiles = rows_dev // tile_rows * across
    tile = lax.broadcasted_iota(jnp.int32, (tiles, LANES), 0)
    pixel = lax.broadcasted_iota(jnp.int32, (tiles, LANES), 1)
    row = first_row + tile // across * tile_rows + pixel // tile_cols
    col = tile % across * tile_cols + pixel % tile_cols
    yy = (row.astype(jnp.float32) + 0.5) / npix * 2.0 - 1.0
    xx = (col.astype(jnp.float32) + 0.5) / npix * 2.0 - 1.0
    dist = jnp.sqrt(xx * xx + yy * yy)
    upos = (dist - R_INNER) / (1.0 - R_INNER) * nrad - 0.5
    floor_u = jnp.floor(upos)
    frac_u = upos - floor_u
    lower = jnp.clip(floor_u.astype(jnp.int32), -2, nrad) + LANES
    angle = jnp.arctan2(yy, xx)
    vpos = (angle + jnp.pi) / (2.0 * jnp.pi) * nphi - 0.5
    window = jnp.min(lower, axis=1) // (LANES // 2)
    window = jnp.clip(window, 0, (nrad + LANES) // (LANES // 2))
    above = jnp.where(first_row >= npix // 2, nphi // 2, 0) - 8
    start = jnp.clip(jnp.floor(jnp.min(vpos, axis=1)).astype(jnp.int32) - above, 0, nphi // 2 + 8)
    spot = jnp.clip(lower - window[:, None] * (LANES // 2), 0, LANES - 2)
    return start, window, spot, frac_u, vpos - (start[:, None] + above).astype(jnp.float32)


def window_rows(rows_dev, npix, nphi):
    tile_rows = min(8, rows_dev)
    tile_cols = LANES // tile_rows
    diagonal = 2.0 * np.hypot(tile_rows, tile_cols) / npix
    span = diagonal / (R_INNER - diagonal) / (2.0 * np.pi) * nphi
    return -(-int(np.ceil(span) + 2) // 8) * 8


def image_kernel(rows, tile_rows, across, start_ref, window_ref, spot_ref, frac_ref, vpos_ref, *refs):
    *table_refs, out_ref, wide_ref = refs
    blocks = len(table_refs)
    tall = table_refs[0].shape[0]
    half = LANES // 2
    windows = 2 * (blocks + 2) - 1
    row = lax.axis_index("row")
    for j in range(blocks):
        block = partner(row, j, blocks)
        value = table_refs[j][...]
        wide_ref[pl.ds(2 * block + 2, tall, stride=windows), :] = value
    zero = jnp.zeros((tall, LANES), jnp.float32)
    wide_ref[pl.ds(0, tall, stride=windows), :] = zero
    wide_ref[pl.ds(windows - 1, tall, stride=windows), :] = zero
    for w in range(1, windows, 2):
        left = wide_ref[pl.ds(w - 1, tall, stride=windows), :]
        right = wide_ref[pl.ds(w + 1, tall, stride=windows), :]
        wide_ref[pl.ds(w, tall, stride=windows), :] = jnp.concatenate([left[:, half:], right[:, :half]], axis=1)

    sub = lax.broadcasted_iota(jnp.int32, (8, LANES), 0)
    lane = lax.broadcasted_iota(jnp.int32, (8, LANES), 1)

    def one_tile(tile):
        start = start_ref[tile]
        at = start * windows + window_ref[tile]
        spot = jnp.broadcast_to(spot_ref[pl.ds(tile, 1), :], (8, LANES))
        frac = jnp.broadcast_to(frac_ref[pl.ds(tile, 1), :], (8, LANES))
        vpos = jnp.broadcast_to(vpos_ref[pl.ds(tile, 1), :], (8, LANES))
        total = None
        for r in range(0, rows, 8):
            block = wide_ref[pl.ds(at + r * windows, 8, stride=windows), :]
            low = jnp.take_along_axis(block, spot, axis=1)
            high = jnp.take_along_axis(block, spot + 1, axis=1)
            weight = jnp.maximum(0.0, 1.0 - jnp.abs((sub + r).astype(jnp.float32) - vpos))
            part = weight * (low + frac * (high - low))
            total = part if total is None else total + part
        return total

    def group(index, carry):
        parts = [one_tile(index * 8 + t) for t in range(8)]
        for d in (4, 2, 1):
            upper = (sub & d) != 0
            parts = [
                jnp.where(upper, b, a) + jnp.where(upper, pltpu.roll(b, d, 0), pltpu.roll(a, 8 - d, 0))
                for a, b in zip(parts[:d], parts[d:])
            ]
        result = parts[0]
        if tile_rows == 8:
            width = LANES // 8
            for d in (1, 2, 4):
                low_sub = (sub & d) == 0
                low_lane = (lane & (d * width)) == 0
                ahead = pltpu.roll(pltpu.roll(result, 8 - d, 0), d * width, 1)
                back = pltpu.roll(pltpu.roll(result, d, 0), LANES - d * width, 1)
                result = jnp.where(low_sub == low_lane, result, jnp.where(low_sub, ahead, back))
            per_row = across // 8
            out_ref[pl.ds(pl.multiple_of(index // per_row * 8, 8), 8), pl.ds(pl.multiple_of(index % per_row * LANES, LANES), LANES)] = result
        else:
            out_ref[pl.ds(pl.multiple_of(index * 8, 8), 8), :] = result
        return carry

    lax.fori_loop(0, spot_ref.shape[0] // 8, group, 0, unroll=min(8, spot_ref.shape[0] // 8))


def draw_image(tables, geometry, rows, rows_dev, npix, nrad):
    start, window, spot, frac_u, vpos = geometry
    tiles = spot.shape[0]
    tile_rows = min(8, rows_dev)
    tile_cols = LANES // tile_rows
    across = npix // tile_cols
    windows = 2 * (nrad // LANES + 2) - 1
    shape = (rows_dev, npix) if tile_rows == 8 else (tiles, LANES)
    image = pl.pallas_call(
        functools.partial(image_kernel, rows, tile_rows, across),
        out_shape=jax.ShapeDtypeStruct(shape, jnp.float32),
        in_specs=smem(2) + vmem(3 + len(tables)),
        out_specs=pl.BlockSpec(memory_space=pltpu.VMEM),
        scratch_shapes=[pltpu.VMEM((tables[0].shape[0] * windows, LANES), jnp.float32)],
        compiler_params=params(),
        name="image",
    )(start, window, spot, frac_u, vpos, *tables)
    if tile_rows == 8:
        return image
    image = image.reshape(rows_dev // tile_rows, across, tile_rows, tile_cols)
    return jnp.swapaxes(image, 1, 2).reshape(rows_dev, npix)


def order(size):
    return ORDER if size == len(ORDER) else tuple(range(size))


def partner(place, index, size):
    return place ^ order(size)[index]


def swapped(piece, axis, index):
    size = lax.axis_size(axis)
    return lax.ppermute(piece, axis, [(p, partner(p, index, size)) for p in range(size)])


def exchange(chunks, axis):
    size = lax.axis_size(axis)
    if size > INNER:
        place, every = lax.axis_index(axis), jnp.arange(size)
        sent = jnp.stack(chunks)[place ^ every]
        got = lax.all_to_all(sent, axis, 0, 0, tiled=True)[place ^ every]
        return [got[i] for i in range(size)]
    return [chunks[0]] + [swapped(chunks[i], axis, i) for i in range(1, size)]


def gather_kernel(cells, cycle, half_rows, cut, *refs):
    *piece_refs, out_ref, light_ref, turned_ref = refs
    count = piece_refs[0].shape[0] - cut
    place = lax.axis_index("phi")
    for j in range(len(piece_refs)):
        at = partner(place, j, len(piece_refs)) * count
        light_ref[pl.ds(pl.multiple_of(at, 8), count), :] = piece_refs[j][pl.ds(cut, count), :]
    for l in range(light_ref.shape[1] // LANES):
        turned_ref[pl.ds(l * LANES, LANES), :] = light_ref[:, pl.ds(l * LANES, LANES)].T

    def slab(index):
        return turned_ref[pl.ds(lax.rem(index + cycle, cycle), cells, stride=cycle), :]

    first = jnp.where(place >= cycle // 2, cycle // 2, 0)
    out_ref[...] = jnp.zeros_like(out_ref)
    for s in range(cycle // 2):
        out_ref[pl.ds(8 + s * cells, cells), :] = slab(first + s)
    out_ref[pl.ds(0, 8), :] = slab(first - 1)[cells - 8:, :]
    out_ref[pl.ds(8 + half_rows, 8), :] = slab(first + cycle // 2)[:8, :]


def neighbour_columns(first, second):
    cycle, bands = lax.axis_size("phi"), lax.axis_size("row")
    order = [q * bands + r for r in range(bands) for q in range(cycle)]
    pairs = list(zip(order[:-1], order[1:]))

    def both_ways(piece, chosen):
        return lax.ppermute(piece, ("phi", "row"), chosen + [(j, i) for i, j in chosen])

    return both_ways(first, pairs[::2]), both_ways(second, pairs[1::2])


def body(density, velocity, shifts, fractions):
    cycle = lax.axis_size("phi")
    bands = lax.axis_size("row")
    cells, polar, radial = density.shape
    groups = polar // INNER
    per_column = FIELDS * groups
    columns = radial // cycle
    nphi = cells * cycle
    nrad = radial * bands
    place = lax.axis_index("phi")
    row = lax.axis_index("row")
    block = (FIELDS, cells, polar, radial)
    shifts, fractions = jnp.clip(shifts, 0, nphi - 1), jnp.clip(fractions, 0.0, 1.0)
    hbm = pl.BlockSpec(memory_space=pltpu.HBM)

    def f32(*shape):
        return jax.ShapeDtypeStruct(shape, jnp.float32)

    chunk = f32(columns * per_column, LANES)
    chunks = pl.pallas_call(
        pack_kernel,
        out_shape=[chunk] * cycle,
        in_specs=[hbm] * 2,
        out_specs=vmem(cycle),
        scratch_shapes=[
            pltpu.VMEM((radial * per_column, LANES), jnp.float32),
            pltpu.VMEM(block, jnp.float32),
            pltpu.SemaphoreType.DMA((FIELDS * SPLIT,)),
        ],
        compiler_params=pltpu.CompilerParams(vmem_limit_bytes=PACK_LIMIT),
        name="pack",
    )(density, velocity)
    ring = exchange(chunks, "phi")
    rows_dev = NPIX // (cycle * bands)
    geometry = pixel_tiles((place * bands + row) * rows_dev, rows_dev, NPIX, nphi, nrad)

    column_rows = per_column * cycle
    edge = HALO * column_rows
    pieces = pl.pallas_call(
        functools.partial(halo_kernel, cycle, columns, len(geometry)),
        out_shape=[f32(edge + 8, LANES)] * 2,
        in_specs=smem(2) + vmem(cycle) + [pl.BlockSpec(memory_space=pl.ANY)] * len(geometry),
        out_specs=vmem(2),
        compiler_params=params(),
        name="halo",
    )(shifts, fractions, *ring, *geometry)
    first, second = neighbour_columns(*pieces)
    theta = (np.arange(polar) + 0.5) / polar
    tilt = (1.0 + 0.5 * np.cos(np.pi * theta)).reshape(INNER, groups).T
    tilt = jnp.asarray(np.tile(tilt, (1, LANES // INNER)), jnp.float32)
    margin = HALO if columns >= INNER else 0
    inner = []
    if margin:
        inner = pl.pallas_call(
            functools.partial(inner_kernel, cells, cycle, columns, nrad, groups, margin),
            out_shape=[
                f32(columns * column_rows, LANES), f32(2 * edge, LANES), f32(-(-columns // INNER), cycle, LANES)
            ],
            in_specs=smem(2) + vmem(1 + cycle),
            out_specs=vmem(3),
            scratch_shapes=[pltpu.VMEM((columns * column_rows, LANES), jnp.float32) for _ in range(2)],
            compiler_params=params(),
            name="inner",
        )(shifts, fractions, tilt, *ring)
    swap = cycle == INNER and columns % INNER == 0
    rows = columns * per_column
    slots = -(-columns // INNER)
    out = pl.pallas_call(
        functools.partial(outer_kernel, cells, cycle, columns, nrad, groups, margin, swap),
        out_shape=[f32(rows + columns, LANES)] * cycle if swap else [f32(rows, LANES)] * cycle + [f32(slots, cycle, LANES)],
        in_specs=smem(2) + vmem(3 + cycle + len(inner)),
        out_specs=vmem(cycle + (not swap)),
        scratch_shapes=[
            pltpu.VMEM((4 * edge, LANES), jnp.float32),
            pltpu.VMEM(((columns + 2 * HALO) * column_rows, LANES), jnp.float32),
            pltpu.VMEM((columns * column_rows, LANES), jnp.float32),
        ],
        compiler_params=params(),
        name="outer",
    )(shifts, fractions, tilt, first, second, *ring, *inner)
    back = exchange(out[:cycle], "phi")
    if swap:
        light_pieces, cut = back, rows
    else:
        light = out[cycle].reshape(slots, cycle, cells, INNER).transpose(0, 3, 2, 1).reshape(slots * INNER, nphi)[:columns]
        light_pieces, cut = [lax.all_gather(light, "phi", axis=0, tiled=True)], 0
    window = window_rows(rows_dev, NPIX, nphi)
    table = pl.pallas_call(
        functools.partial(gather_kernel, cells, cycle, nphi // 2, cut),
        out_shape=f32(nphi // 2 + 16 + window, LANES),
        in_specs=vmem(len(light_pieces)),
        out_specs=pl.BlockSpec(memory_space=pltpu.VMEM),
        scratch_shapes=[pltpu.VMEM((radial, nphi), jnp.float32), pltpu.VMEM((nphi, LANES), jnp.float32)],
        compiler_params=params(),
        name="gather",
    )(*light_pieces)
    tables = exchange([table] * bands, "row")

    density_out, velocity_out = pl.pallas_call(
        unpack_kernel,
        out_shape=(f32(*density.shape), f32(*velocity.shape)),
        in_specs=vmem(cycle),
        out_specs=[hbm] * 2,
        scratch_shapes=[
            pltpu.VMEM((radial * per_column, LANES), jnp.float32),
            pltpu.VMEM(block, jnp.float32),
            pltpu.SemaphoreType.DMA((FIELDS * SPLIT,)),
        ],
        compiler_params=params(),
        name="unpack",
    )(*back)

    image = draw_image(tables, geometry, window, rows_dev, NPIX, nrad)
    return (density_out, velocity_out, image)


def solution(mesh):
    in_specs = (P("phi", None, "row"), P(None, "phi", None, "row"), P("row"), P("row"))
    out_specs = (P("phi", None, "row"), P(None, "phi", None, "row"), P(("phi", "row"), None))
    return jax.shard_map(body, mesh=mesh, in_specs=in_specs, out_specs=out_specs, check_vma=False)
```
